512 devices in a mesh: section: 32 (over x_lo, z), tensor: 16 (over y, x_hi, core).
Axes of the slice: x: 4 (x_hi: 2, x_lo: 2; x = x_hi * 2 + x_lo), y: 4, z: 16, core: 2. Of those that a mesh axis runs over, the one named last changes fastest.
Arguments:
- section_input: bfloat16 [32, 128, 3072], P('section', 'tensor'), may hold values from -6 to 6
- query: bfloat16 [32, 3072, 128], P('section', 'tensor'), may hold values from -100 to 100
- key_stash: bfloat16 [32, 3072, 128], P('section', 'tensor'), may hold values from -4 to 4
- incoming: bfloat16 [32, 128, 3072], P('section', 'tensor'), may hold values from -6 to 6
- version: int32 [32], P('section'), may hold values from 0 to 1
- w_value: bfloat16 [32, 2, 3072, 1536], P('section', None, 'tensor'), may hold values from -0.109375 to 0.109375
- w_out: bfloat16 [32, 2, 3072, 1536], P('section', None, 'tensor'), may hold values from -0.109375 to 0.109375
Outputs:
- input_grad: bfloat16 [32, 128, 3072], P('section', 'tensor')
- grad_value: bfloat16 [32, 3072, 1536], P('section', 'tensor')
- grad_out: bfloat16 [32, 3072, 1536], P('section', 'tensor')
The draws below stay inside these ranges and needn't reach their ends.
All inputs are finite; a program needn't handle non-finite values.
Results may differ from the reference program's by a relative error of at most 0.018.
Values may be sent and summed in bfloat16 or wider, within the bound.
A program may use at most 64 MiB of HBM per device.

```python
import math
import jax
import jax.numpy as jnp
from jax import lax

D = 3072
HEADS = 32
HEAD_DIM = 96
TOKENS = 128
ATTN = 3072
SLOTS = 32
N_TENSOR = 16


def stash_base(key):
    base_key = jax.random.fold_in(key, 5)
    return jnp.clip(jax.random.normal(base_key, (SLOTS, ATTN, TOKENS), jnp.float32), -4.0, 4.0)


def draw_query(key, part):
    base = stash_base(key)
    key = jax.random.fold_in(key, 21)
    drawn = jnp.clip(jax.random.normal(key, base.shape, jnp.float32), -4.0, 4.0)
    return drawn.astype(jnp.bfloat16)


def draw_key_stash(key, part):
    base = stash_base(key)
    drawn = base
    return drawn.astype(jnp.bfloat16)


def place_ends(values, rng, smallest, top_value):
    spot = [jax.random.randint(jax.random.fold_in(rng, axis), (), 0, length) for axis, length in enumerate(values.shape)]
    widest = values.shape.index(max(values.shape))
    beside = spot[:widest] + [(spot[widest] + 1) % values.shape[widest]] + spot[widest + 1:]
    return values.at[tuple(spot)].set(smallest).at[tuple(beside)].set(top_value)


def block_scale(own_key, shape, cuts, low, largest):
    factor_of = 1.0
    for dim, shards_of in cuts:
        draws = jax.random.uniform(jax.random.fold_in(jax.random.fold_in(own_key, 6), dim), (shards_of,), jnp.float32, low / len(cuts), largest / len(cuts))
        factor_of = factor_of * jnp.repeat(jnp.exp(draws), shape[dim] // shards_of).reshape((-1,) + (1,) * (len(shape) - 1 - dim))
    return factor_of


def normal_values(key, extent, scale, reach, shards=(), dtype=jnp.bfloat16):
    values = scale * jax.random.normal(key, extent, jnp.float32)
    if shards:
        values = values * block_scale(key, extent, shards, -0.22, 0.18)
    return jnp.clip(values, -reach, reach).astype(dtype)


def setup_inputs(seed: int = 0) -> dict:
    seeds = jax.random.split(jax.random.key(seed), 8)
    return {
        "section_input": normal_values(seeds[0], (SLOTS, TOKENS, D), 1.0, 6.0, ((0, 32), (1, 16))),
        "query": draw_query(jax.random.fold_in(seeds[7], 71), 0),
        "key_stash": draw_key_stash(jax.random.fold_in(seeds[7], 71), 0),
        "incoming": normal_values(seeds[3], (SLOTS, TOKENS, D), 1.0, 6.0, ((0, 32), (1, 16))),
        "version": place_ends(jax.random.randint(seeds[4], (SLOTS,), 0, 2), jax.random.fold_in(seeds[4], 1), 0, 1).astype(jnp.int32),
        "w_value": normal_values(seeds[5], (SLOTS, 2, ATTN, D // 2), D ** -0.5, 0.109375, ((0, 32), (2, 16))),
        "w_out": normal_values(seeds[6], (SLOTS, 2, ATTN, D // 2), ATTN ** -0.5, 0.109375, ((0, 32), (2, 16))),
    }


def attention_probs(query, key_stash):
    query_heads = query.astype(jnp.float32).reshape(HEADS, HEAD_DIM, TOKENS)
    key_heads = key_stash.astype(jnp.float32).reshape(HEADS, HEAD_DIM, TOKENS)
    scores = jnp.einsum('hdi,hdj->hij', query_heads, key_heads) * (1.0 / math.sqrt(HEAD_DIM))
    causal = lax.broadcasted_iota(jnp.int32, (TOKENS, TOKENS), 1) <= lax.broadcasted_iota(jnp.int32, (TOKENS, TOKENS), 0)
    scores = jnp.where(causal, scores, -jnp.inf)
    row_max = lax.optimization_barrier(jnp.max(scores, axis=2, keepdims=True))
    expo = jnp.exp(scores - row_max)
    return (expo / lax.optimization_barrier(jnp.sum(expo, axis=2, keepdims=True))).astype(jnp.bfloat16)

def section_backward(inputs, query, key_stash, value_weight, out_weight, upstream_grad):
    values = jnp.dot(value_weight, inputs.T, preferred_element_type=jnp.float32).astype(jnp.bfloat16)
    attend = attention_probs(query, key_stash).astype(jnp.float32)
    value_heads = values.astype(jnp.float32).reshape(HEADS, HEAD_DIM, TOKENS)
    context = jnp.einsum('hdj,hij->hdi', value_heads, attend).astype(jnp.bfloat16).reshape(ATTN, TOKENS)
    context_grad = jnp.dot(out_weight, upstream_grad.T, preferred_element_type=jnp.float32).astype(jnp.bfloat16)
    context_heads = context_grad.astype(jnp.float32).reshape(HEADS, HEAD_DIM, TOKENS)
    value_grad = jnp.einsum('hdi,hij->hdj', context_heads, attend).astype(jnp.bfloat16).reshape(ATTN, TOKENS)
    grad_groups = value_grad.astype(jnp.float32).reshape(N_TENSOR, ATTN // N_TENSOR, TOKENS)
    weight_groups = value_weight.astype(jnp.float32).reshape(N_TENSOR, ATTN // N_TENSOR, D)
    partials = jnp.einsum('gat,gad->gtd', grad_groups, weight_groups).astype(jnp.bfloat16)
    partials = lax.optimization_barrier(partials).astype(jnp.float32)
    input_grad = (upstream_grad.astype(jnp.float32) + lax.optimization_barrier(jnp.sum(partials, axis=0))).astype(jnp.bfloat16)
    value_wgrad = jnp.dot(value_grad, inputs, preferred_element_type=jnp.float32)
    out_wgrad = jnp.dot(context, upstream_grad, preferred_element_type=jnp.float32)
    return (input_grad, value_wgrad, out_wgrad)

def section_weights(table, slot_index, chosen):
    pair_index = slot_index // 2
    return jnp.concatenate([table[2 * pair_index][chosen], table[2 * pair_index + 1][chosen]], axis=-1)

def reference(section_input, query, key_stash, incoming, version, w_value, w_out):
    grads_in = [None] * SLOTS
    value_wgrads = [None] * SLOTS
    out_wgrads = [None] * SLOTS
    order = [slot for slot in range(SLOTS) if slot // 2 % 2 == 1] + [slot for slot in range(SLOTS) if slot // 2 % 2 == 0]
    for slot_index in order:
        chosen = version[slot_index]
        value_weight = section_weights(w_value, slot_index, chosen)
        out_weight = section_weights(w_out, slot_index, chosen)
        if slot_index // 2 % 2 == 1:
            upstream_grad = incoming[slot_index]
        else:
            upstream_grad = grads_in[slot_index + 2]
        result = section_backward(section_input[slot_index], query[slot_index], key_stash[slot_index], value_weight, out_weight, upstream_grad)
        grads_in[slot_index], value_wgrads[slot_index], out_wgrads[slot_index] = result
    half_width = D // 2
    value_parts = []
    out_parts = []
    for pair_index in range(SLOTS // 2):
        value_total = value_wgrads[2 * pair_index] + value_wgrads[2 * pair_index + 1]
        out_total = out_wgrads[2 * pair_index] + out_wgrads[2 * pair_index + 1]
        value_parts.append(value_total[:, :half_width].astype(jnp.bfloat16))
        value_parts.append(value_total[:, half_width:].astype(jnp.bfloat16))
        out_parts.append(out_total[:, :half_width].astype(jnp.bfloat16))
        out_parts.append(out_total[:, half_width:].astype(jnp.bfloat16))
    return (jnp.stack(grads_in), jnp.stack(value_parts), jnp.stack(out_parts))
```

```python
import functools
import math

import jax
import jax.numpy as jnp
from jax import lax
from jax.experimental import pallas as pl
from jax.experimental.pallas import tpu as pltpu
from jax.sharding import PartitionSpec as P

HEAD_DIM = 96
BF16 = jnp.bfloat16
F32 = jnp.float32
MESH = pl.DeviceIdType.MESH


def dot(left, right, left_dim, right_dim):
    return lax.dot_general(
        left, right, (((left_dim,), (right_dim,)), ((), ())), preferred_element_type=F32
    )


def kernel(
    count,
    x_ref, query_ref, key_ref, incoming_ref, version_ref, wv_ref, wo_ref,
    dx_ref, gv_ref, go_ref,
    wv, wo, query, key, probs, versions,
    grad_own, grad_in, x_in, grad_full, x_full,
    values_own, values_sent, values_got, grads_own, grads_sent, grads_got,
    context, value_grad, dx_parts, dx_got, dx_own, gv, go,
    load_sem, pair_send, pair_recv, x_send, x_recv, grad_send, grad_recv,
    dx_send, dx_recv, shift_send, shift_recv, out_sem,
):
    section = lax.axis_index("section")
    tensor = lax.axis_index("tensor")
    mine = lax.rem(section, 2)
    base = section - mine
    partner = base + 1 - mine
    odd = lax.rem(section // 2, 2)
    other = section + 2 - 4 * odd
    rows = wv.shape[1]
    half = wv.shape[2]
    heads = rows // HEAD_DIM
    shard = grad_own.shape[0]
    tokens = count * shard
    tile = half // 3 if half % 384 == 0 else half
    own_slot = mine * count + tensor

    def peer(step):
        return lax.rem(tensor + step, count)

    def columns(which):
        return pl.ds(pl.multiple_of(which * half, half), half)

    loads = [
        pltpu.make_async_copy(query_ref.at[0], query, load_sem.at[0]),
        pltpu.make_async_copy(key_ref.at[0], key, load_sem.at[1]),
        pltpu.make_async_copy(wo_ref.at[0], wo, load_sem.at[2]),
        pltpu.make_async_copy(wv_ref.at[0], wv, load_sem.at[3]),
    ]
    own_load = pltpu.make_async_copy(incoming_ref.at[0], grad_own, load_sem.at[4])
    for load in loads:
        load.start()
    pl.when(odd == 1)(own_load.start)

    barrier = pltpu.get_barrier_semaphore()

    def greet(target, first):
        def step(j, carry):
            pl.semaphore_signal(
                barrier, inc=1, device_id=(target, peer(j)), device_id_type=MESH
            )
            return carry

        lax.fori_loop(first, count, step, 0)

    pl.semaphore_signal(barrier, inc=1, device_id=(other, tensor), device_id_type=MESH)
    greet(section, 1)
    greet(partner, 0)
    pl.semaphore_wait(barrier, 2 * count)

    def send_to(target, first, source, destination, send, recv):
        def step(j, carry):
            pltpu.make_async_remote_copy(
                src_ref=source(peer(j)),
                dst_ref=destination,
                send_sem=send,
                recv_sem=recv,
                device_id=(target, peer(j)),
                device_id_type=MESH,
            ).start()
            return carry

        lax.fori_loop(first, count, step, 0)

    def gather_start(source, buffer, send, recv):
        slot = buffer.at[own_slot]
        send_to(section, 1, lambda _: source.at[:, columns(mine)], slot, send, recv)
        send_to(partner, 0, lambda _: source.at[:, columns(1 - mine)], slot, send, recv)
        pltpu.make_async_copy(source.at[:, columns(mine)], slot, recv).start()

    def wait_all(buffer, sem):
        pltpu.make_async_copy(buffer, buffer, sem).wait()

    def wait_sent(buffer, sem):
        sent = buffer.at[pl.ds(0, 2 * count - 1)]
        pltpu.make_async_copy(sent, sent, sem).wait()

    def flatten(buffer, full):
        def step(i, carry):
            block = buffer[pl.ds(2 * i, 2)].astype(F32).reshape(2 * shard, half)
            full[pl.ds(pl.multiple_of(i * 2 * shard, 2 * shard), 2 * shard), :] = block.astype(BF16)
            return carry

        lax.fori_loop(0, count, step, 0)

    def to_partner(source, destination, index):
        return pltpu.make_async_remote_copy(
            src_ref=source,
            dst_ref=destination,
            send_sem=pair_send.at[index],
            recv_sem=pair_recv.at[index],
            device_id=(partner, tensor),
            device_id_type=MESH,
        )

    send_probs = to_partner(probs.at[mine], probs.at[mine], 0)
    send_version = to_partner(versions.at[mine], versions.at[mine], 1)
    send_values = to_partner(values_sent, values_got, 2)
    send_grads = to_partner(grads_sent, grads_got, 3)
    shift = pltpu.make_async_remote_copy(
        src_ref=dx_own,
        dst_ref=grad_own,
        send_sem=shift_send,
        recv_sem=shift_recv,
        device_id=(other, tensor),
        device_id_type=MESH,
    )

    def attention():
        versions[mine] = jnp.full(versions.shape[1:], version_ref[0], jnp.int32)
        send_version.start()
        loads[0].wait()
        loads[1].wait()
        row = lax.broadcasted_iota(jnp.int32, (tokens, tokens), 0)
        causal = lax.broadcasted_iota(jnp.int32, (tokens, tokens), 1) <= row
        for head in range(heads):
            part = slice(head * HEAD_DIM, (head + 1) * HEAD_DIM)
            scores = dot(query[part], key[part], 0, 0) * (1.0 / math.sqrt(HEAD_DIM))
            scores = jnp.where(causal, scores, -jnp.inf)
            expo = jnp.exp(scores - jnp.max(scores, axis=1, keepdims=True))
            attend = expo / jnp.sum(expo, axis=1, keepdims=True)
            probs[mine, head] = attend.astype(BF16)
        send_probs.start()
        send_version.wait()
        send_probs.wait()
        loads[2].wait()
        loads[3].wait()

    def chosen(which):
        return jnp.max(versions[which])

    def token_rows(which):
        return slice(which * tokens, (which + 1) * tokens)

    def project(weight, full, own, sent):
        for which in range(2):
            partial = dot(weight[chosen(which)], full[token_rows(which)], 1, 1)
            own[which] = partial
            sent[which] = partial.astype(BF16)

    def mix(own, got, out, side):
        for which in range(2):
            for head in range(heads):
                part = slice(head * HEAD_DIM, (head + 1) * HEAD_DIM)
                whole = (own[which, part] + got[which, part].astype(F32)).astype(BF16)
                mixed = dot(whole, probs[which, head], 1, side)
                out[part, token_rows(which)] = mixed.astype(BF16)

    def forward_half():
        gather_start(x_ref.at[0], x_in, x_send, x_recv)

    def context_phase():
        wait_all(x_in, x_recv)
        flatten(x_in, x_full)
        project(wv, x_full, values_own, values_sent)
        send_values.start()
        send_values.wait()
        mix(values_own, values_got, context, 1)

    def gradient_phase():
        wait_all(grad_in, grad_recv)
        flatten(grad_in, grad_full)
        project(wo, grad_full, grads_own, grads_sent)
        send_grads.start()
        send_grads.wait()
        mix(grads_own, grads_got, value_grad, 0)
        for which in range(2):
            weight = wv.at[chosen(which)]
            for start in range(0, half, tile):
                part = dot(value_grad[:, token_rows(which)], weight[:, start:start + tile], 0, 0)
                dx_parts[which * count:(which + 1) * count, :, start:start + tile] = part.reshape(
                    count, shard, tile
                ).astype(BF16)
            send_to(
                base + which,
                jnp.where(mine == which, 1, 0),
                lambda to: dx_parts.at[which * count + to],
                dx_got.at[own_slot],
                dx_send,
                dx_recv,
            )
        pltpu.make_async_copy(dx_parts.at[own_slot], dx_got.at[own_slot], dx_recv).start()

    def reduce_phase():
        wait_all(dx_got, dx_recv)
        for side in range(2):
            part = slice(side * half, (side + 1) * half)
            total = dx_got[side * count].astype(F32)
            for slot in range(1, count):
                total = total + dx_got[side * count + slot].astype(F32)
            dx_own[:, part] = (grad_own[:, part].astype(F32) + total).astype(BF16)
        pltpu.make_async_copy(dx_own, dx_ref.at[0], out_sem.at[0]).start()

    def weight_phase():
        for start in range(0, half, tile):
            part = slice(start, start + tile)
            gv[:, part] = dot(value_grad[...], x_full[:, part], 1, 0).astype(BF16)
        pltpu.make_async_copy(gv, gv_ref.at[0], out_sem.at[1]).start()
        for start in range(0, half, tile):
            part = slice(start, start + tile)
            go[:, part] = dot(context[...], grad_full[:, part], 1, 0).astype(BF16)
        pltpu.make_async_copy(go, go_ref.at[0], out_sem.at[2]).start()

    def odd_section():
        gather_start(incoming_ref.at[0], grad_in, grad_send, grad_recv)
        attention()
        gradient_phase()
        own_load.wait()
        reduce_phase()
        shift.start()
        forward_half()
        context_phase()
        weight_phase()
        shift.wait_send()

    def even_section():
        forward_half()
        attention()
        context_phase()
        shift.wait_recv()
        gather_start(grad_own, grad_in, grad_send, grad_recv)
        gradient_phase()
        weight_phase()
        reduce_phase()

    pl.when(odd == 1)(odd_section)
    pl.when(odd == 0)(even_section)
    wait_sent(x_in, x_send)
    wait_sent(grad_in, grad_send)
    wait_sent(dx_parts, dx_send)
    pltpu.make_async_copy(dx_own, dx_ref.at[0], out_sem.at[0]).wait()
    pltpu.make_async_copy(gv, gv_ref.at[0], out_sem.at[1]).wait()
    pltpu.make_async_copy(go, go_ref.at[0], out_sem.at[2]).wait()


def on_device(section_input, query, key_stash, incoming, version, w_value, w_out):
    count = lax.axis_size("tensor")
    shard, width = section_input.shape[1:]
    rows, tokens = query.shape[1:]
    half = width // 2
    heads = rows // HEAD_DIM
    anywhere = pl.BlockSpec(memory_space=pl.ANY)
    pair = (2, rows, tokens)
    blocks = (2 * count, shard, half)
    dma = pltpu.SemaphoreType.DMA
    return pl.pallas_call(
        functools.partial(kernel, count),
        out_shape=(
            jax.ShapeDtypeStruct((1, shard, width), BF16),
            jax.ShapeDtypeStruct((1, rows, half), BF16),
            jax.ShapeDtypeStruct((1, rows, half), BF16),
        ),
        in_specs=[anywhere] * 4 + [pl.BlockSpec(memory_space=pltpu.SMEM)] + [anywhere] * 2,
        out_specs=(anywhere, anywhere, anywhere),
        scratch_shapes=[
            pltpu.VMEM((2, rows, half), BF16),
            pltpu.VMEM((2, rows, half), BF16),
            pltpu.VMEM((rows, tokens), BF16),
            pltpu.VMEM((rows, tokens), BF16),
            pltpu.VMEM((2, heads, tokens, tokens), BF16),
            pltpu.VMEM((2, 8, 128), jnp.int32),
            pltpu.VMEM((shard, width), BF16),
            pltpu.VMEM(blocks, BF16),
            pltpu.VMEM(blocks, BF16),
            pltpu.VMEM((2 * tokens, half), BF16),
            pltpu.VMEM((2 * tokens, half), BF16),
            pltpu.VMEM(pair, F32),
            pltpu.VMEM(pair, BF16),
            pltpu.VMEM(pair, BF16),
            pltpu.VMEM(pair, F32),
            pltpu.VMEM(pair, BF16),
            pltpu.VMEM(pair, BF16),
            pltpu.VMEM((rows, 2 * tokens), BF16),
            pltpu.VMEM((rows, 2 * tokens), BF16),
            pltpu.VMEM(blocks, BF16),
            pltpu.VMEM(blocks, BF16),
            pltpu.VMEM((shard, width), BF16),
            pltpu.VMEM((rows, half), BF16),
            pltpu.VMEM((rows, half), BF16),
            dma((5,)),
            dma((4,)),
            dma((4,)),
            dma,
            dma,
            dma,
            dma,
            dma,
            dma,
            dma,
            dma,
            dma((3,)),
        ],
        compiler_params=pltpu.CompilerParams(
            collective_id=0, has_side_effects=True, vmem_limit_bytes=40 * 1024 * 1024
        ),
    )(section_input, query, key_stash, incoming, version, w_value, w_out)


def solution(mesh):
    split = P("section", "tensor", None)
    weights = P("section", None, "tensor", None)
    return jax.shard_map(
        on_device,
        mesh=mesh,
        in_specs=(split, split, split, split, P("section"), weights, weights),
        out_specs=(split, split, split),
        check_vma=False,
    )
```

```python
import functools
import math

import jax
import jax.numpy as jnp
from jax import lax
from jax.experimental import pallas as pl
from jax.experimental.pallas import tpu as pltpu
from jax.sharding import PartitionSpec as P

HEAD_DIM = 96
BF16 = jnp.bfloat16
F32 = jnp.float32
MESH = pl.DeviceIdType.MESH


def dot(left, right, left_dim, right_dim):
    return lax.dot_general(
        left, right, (((left_dim,), (right_dim,)), ((), ())), preferred_element_type=F32
    )


def kernel(
    count,
    x_ref, query_ref, key_ref, incoming_ref, version_ref, wv_ref, wo_ref,
    dx_ref, gv_ref, go_ref,
    wv, wo, query, key, probs, versions,
    x_in, grad_in, x_full, grad_full,
    part_x, cast_x, sib_x, total_x, sent_x, got_x, context,
    part_g, cast_g, sib_g, total_g, sent_g, got_g, value_grad,
    parts_odd, got_odd, parts_even, got_even,
    reduced, shifted, pieces, assembled, dx_own, grad_own, gv, go, gv_sent, go_sent,
    load_sem, pair_send, pair_recv, sib_send, sib_recv,
    x_send, x_recv, grad_send, grad_recv, dx_send, dx_recv,
    shift_send, shift_recv, piece_send, piece_recv, own_send, own_recv, out_sem,
):
    section = lax.axis_index("section")
    tensor = lax.axis_index("tensor")
    mine = lax.rem(section, 2)
    base = section - mine
    partner = base + 1 - mine
    odd = lax.rem(section // 2, 2)
    other = section + 2 - 4 * odd
    core = lax.rem(tensor, 2)
    chip = tensor // 2
    sibling = tensor + 1 - 2 * core
    rows = wv.shape[1] // 2
    quarter = wv.shape[2]
    half = 2 * quarter
    heads = rows // HEAD_DIM
    shard = grad_own.shape[0]
    tokens = count * shard
    chips = count // 2
    block = 2 * shard
    own_rows = pl.ds(pl.multiple_of(core * rows, 16), rows)
    sib_rows = pl.ds(pl.multiple_of((1 - core) * rows, 16), rows)

    offsets = [(dy, dx) for dx in (1, 0) for dy in sorted(range(chips // 2), key=lambda d: (-min(d, chips // 2 - d), d))]

    def chip_at(dy, dx):
        side = lax.rem(chip, 2)
        return 2 * lax.rem(chip // 2 + dy, chips // 2) + (1 - side if dx else side)

    def columns(side, which):
        return pl.ds(pl.multiple_of(side * half + which * quarter, 128), quarter)

    def remote(source, destination, send, recv, target, lane):
        return pltpu.make_async_remote_copy(
            src_ref=source,
            dst_ref=destination,
            send_sem=send,
            recv_sem=recv,
            device_id=(target, lane),
            device_id_type=MESH,
        )

    def to_partner(source, destination, index):
        return remote(
            source, destination, pair_send.at[index], pair_recv.at[index], partner, tensor
        )

    def to_sibling(source, destination, index):
        return remote(
            source, destination, sib_send.at[index], sib_recv.at[index], section, sibling
        )

    def wait_all(buffer, sem):
        pltpu.make_async_copy(buffer, buffer, sem).wait()

    loads = [
        pltpu.make_async_copy(query_ref.at[0], query, load_sem.at[0]),
        pltpu.make_async_copy(key_ref.at[0], key, load_sem.at[1]),
        pltpu.make_async_copy(
            wo_ref.at[0, :, :, columns(0, core)], wo.at[:, own_rows], load_sem.at[2]
        ),
        pltpu.make_async_copy(
            wv_ref.at[0, :, :, columns(0, core)], wv.at[:, own_rows], load_sem.at[3]
        ),
    ]
    for load in loads:
        load.start()
    versions[mine] = jnp.full(versions.shape[1:], version_ref[0], jnp.int32)

    barrier = pltpu.get_barrier_semaphore()

    def signal(target, lane):
        pl.semaphore_signal(barrier, inc=1, device_id=(target, lane), device_id_type=MESH)

    def greet(target, first):
        def step(j, carry):
            signal(target, lax.rem(tensor + j, count))
            return carry

        lax.fori_loop(first, count, step, 0)

    signal(other, tensor)
    greet(partner, 0)
    greet(section, 1)
    pl.semaphore_wait(barrier, 2 * count)

    send_version = to_partner(versions.at[mine], versions.at[mine], 0)
    send_probs = to_partner(probs.at[mine], probs.at[mine], 1)
    send_wo = to_sibling(wo_ref.at[0, :, :, columns(0, 1 - core)], wo.at[:, own_rows], 0)
    send_wv = to_sibling(wv_ref.at[0, :, :, columns(0, 1 - core)], wv.at[:, own_rows], 1)

    def gather_start(source, buffer, send, recv):
        slot = buffer.at[mine * count + tensor]
        for dy, dx in offsets:
            for swap in (1, 0):
                lane_core = 1 - core if swap else core
                lane = 2 * chip_at(dy, dx) + lane_core
                remote(
                    source.at[:, columns(1 - mine, lane_core)], slot, send, recv.at[mine], partner, lane
                ).start()
        for dy, dx in offsets:
            for swap in (1, 0):
                if dy or dx or swap:
                    lane_core = 1 - core if swap else core
                    lane = 2 * chip_at(dy, dx) + lane_core
                    remote(
                        source.at[:, columns(mine, lane_core)], slot, send, recv.at[mine], section, lane
                    ).start()
        pltpu.make_async_copy(source.at[:, columns(mine, core)], slot, recv.at[mine]).start()

    def gather_wait(buffer, full, recv, which):
        wait_all(buffer.at[pl.ds(which * count, count)], recv.at[which])

        def step(i, carry):
            pair = buffer[pl.ds(which * count + 2 * i, 2)].astype(F32).reshape(block, quarter)
            start = pl.multiple_of(which * tokens + i * block, block)
            full[pl.ds(start, block), :] = pair.astype(BF16)
            return carry

        lax.fori_loop(0, chips, step, 0, unroll=True)

    def gather_sent(buffer, send):
        wait_all(buffer.at[pl.ds(0, 2 * count - 1)], send)

    def attention():
        send_version.start()
        send_wo.start()
        send_wv.start()
        loads[0].wait()
        loads[1].wait()
        row = lax.broadcasted_iota(jnp.int32, (tokens, tokens), 0)
        causal = lax.broadcasted_iota(jnp.int32, (tokens, tokens), 1) <= row
        for head in range(heads):
            part = slice(head * HEAD_DIM, (head + 1) * HEAD_DIM)
            scores = dot(query[part], key[part], 0, 0) * (1.0 / math.sqrt(HEAD_DIM))
            scores = jnp.where(causal, scores, -jnp.inf)
            expo = jnp.exp(scores - jnp.max(scores, axis=1, keepdims=True))
            attend = expo / jnp.sum(expo, axis=1, keepdims=True)
            probs[mine, head] = attend.astype(BF16)
        send_probs.start()
        for load in loads[2:]:
            load.wait()
        send_wo.wait_recv()
        send_wv.wait_recv()
        send_version.wait_recv()
        return [jnp.max(versions[which]) for which in range(2)]

    def token_rows(which):
        return slice(which * tokens, (which + 1) * tokens)

    def chain(weight, full, part, cast, sib, total, sent, got, out, side, first_sib, first_pair):
        def first_copy(which):
            return to_sibling(cast.at[which, sib_rows], sib.at[which], first_sib + which)

        def second_copy(which):
            return to_partner(sent.at[which], got.at[which], first_pair + which)

        def third_copy(which):
            place = out.at[own_rows, token_rows(which)]
            return to_sibling(place, place, first_sib + 2 + which)

        def first(which, version):
            product = dot(weight[version], full[token_rows(which)], 1, 1)
            part[which] = product
            cast[which] = product.astype(BF16)
            first_copy(which).start()

        def second(which):
            first_copy(which).wait_recv()
            chip_sum = part[which, own_rows] + sib[which].astype(F32)
            total[which] = chip_sum
            sent[which] = chip_sum.astype(BF16)
            second_copy(which).start()

        def third(which):
            second_copy(which).wait_recv()
            for head in range(heads):
                block_rows = slice(head * HEAD_DIM, (head + 1) * HEAD_DIM)
                whole = total[which, block_rows] + got[which, block_rows].astype(F32)
                mixed = dot(whole.astype(BF16), probs[which, head], 1, side)
                start = pl.multiple_of(core * rows + head * HEAD_DIM, 16)
                out[pl.ds(start, HEAD_DIM), token_rows(which)] = mixed.astype(BF16)
            third_copy(which).start()

        def last(which):
            third_copy(which).wait_recv()

        def sent_wait():
            for which in range(2):
                first_copy(which).wait_send()
                second_copy(which).wait_send()
                third_copy(which).wait_send()

        return first, second, third, last, sent_wait

    x_chain = chain(
        wv, x_full, part_x, cast_x, sib_x, total_x, sent_x, got_x, context, 1, 2, 2
    )
    grad_chain = chain(
        wo, grad_full, part_g, cast_g, sib_g, total_g, sent_g, got_g, value_grad, 0, 6, 4
    )

    def context_phase(chosen, before_third=lambda: None):
        first, second, third, last, _ = x_chain
        for which in range(2):
            gather_wait(x_in, x_full, x_recv, which)
            first(which, chosen[which])
        for which in range(2):
            second(which)
        before_third()
        for which in range(2):
            third(which)
        for which in range(2):
            last(which)

    def gradient_phase(chosen, arrive, deliver, before_third=lambda: None):
        first, second, third, last, _ = grad_chain
        for which in range(2):
            arrive(which)
            first(which, chosen[which])
        for which in range(2):
            second(which)
        before_third()
        for which in range(2):
            third(which)
        for which in range(2):
            last(which)
            deliver(
                which, dot(value_grad[:, token_rows(which)], wv[chosen[which]], 0, 0)
            )

    send_gv = to_sibling(gv_sent, gv_ref.at[0, :, columns(0, core)], 10)
    send_go = to_sibling(go_sent, go_ref.at[0, :, columns(0, core)], 11)
    store_gv = pltpu.make_async_copy(gv, gv_ref.at[0, :, columns(0, core)], out_sem.at[1])
    store_go = pltpu.make_async_copy(go, go_ref.at[0, :, columns(0, core)], out_sem.at[2])
    store_dx = pltpu.make_async_copy(dx_own, dx_ref.at[0], out_sem.at[0])

    def weight_phase():
        for terms, full, kept, sent, store, send in (
            (value_grad, x_full, gv, gv_sent, store_gv, send_gv),
            (context, grad_full, go, go_sent, store_go, send_go),
        ):
            sent[...] = dot(terms[sib_rows], full[...], 1, 0).astype(BF16)
            send.start()
            kept[...] = dot(terms[own_rows], full[...], 1, 0).astype(BF16)
            store.start()

    def chip_rows(which, place):
        return pl.ds(pl.multiple_of(which * tokens + place * block, block), block)

    def shift(which):
        return remote(
            reduced.at[which], shifted.at[which],
            shift_send.at[which], shift_recv.at[which], other, tensor,
        )

    def hand_over():
        return remote(dx_own, grad_own, own_send, own_recv, other, tensor)

    def quarter_columns(place):
        return slice(place * quarter, (place + 1) * quarter)

    def odd_section():
        gather_start(incoming_ref.at[0], grad_in, grad_send, grad_recv)
        chosen = attention()

        def arrive(which):
            gather_wait(grad_in, grad_full, grad_recv, which)

        def deliver(which, product):
            parts_odd[token_rows(which)] = product.astype(BF16)
            slot = got_odd.at[which * chips + chip]
            for dy, dx in offsets:
                place = chip_at(dy, dx)
                source = parts_odd.at[chip_rows(which, place)]
                if dy or dx:
                    remote(
                        source, slot, dx_send, dx_recv.at[which], section, 2 * place + core
                    ).start()
                else:
                    pltpu.make_async_copy(source, slot, dx_recv.at[which]).start()

        gradient_phase(chosen, arrive, deliver, send_probs.wait_recv)
        for which in range(2):
            wait_all(got_odd.at[pl.ds(which * chips, chips)], dx_recv.at[which])
            total = got_odd[which * chips].astype(F32)
            for place in range(1, chips):
                total = total + got_odd[which * chips + place].astype(F32)
            total = total + grad_full[chip_rows(which, chip), :].astype(F32)
            result = total.astype(BF16)
            reduced[which] = result
            shift(which).start()
            pieces[which] = total.reshape(2, shard, quarter).astype(BF16)
        gather_start(x_ref.at[0], x_in, x_send, x_recv)
        slot = assembled.at[2 * mine + core]
        pltpu.make_async_copy(pieces.at[mine, core], slot, piece_recv).start()
        for target, line, lane, lane_core in (
            (section, mine, sibling, 1 - core),
            (partner, 1 - mine, tensor, core),
            (partner, 1 - mine, sibling, 1 - core),
        ):
            remote(pieces.at[line, lane_core], slot, piece_send, piece_recv, target, lane).start()
        wait_all(assembled, piece_recv)
        for place in range(4):
            dx_own[:, quarter_columns(place)] = assembled[place]
        store_dx.start()
        hand_over().start()
        context_phase(chosen)
        weight_phase()
        gather_sent(grad_in, grad_send)
        wait_all(got_odd.at[pl.ds(0, 2 * chips - 2)], dx_send)
        for which in range(2):
            shift(which).wait_send()
        wait_all(assembled.at[pl.ds(0, 3)], piece_send)
        hand_over().wait_send()

    def even_section():
        gather_start(x_ref.at[0], x_in, x_send, x_recv)
        chosen = attention()
        context_phase(chosen, send_probs.wait_recv)
        for which in range(2):
            shift(which).wait_recv()
            slot = grad_full.at[chip_rows(which, chip)]
            for dy, dx in offsets:
                if dy or dx:
                    remote(
                        shifted.at[which], slot, grad_send, grad_recv.at[which],
                        section, 2 * chip_at(dy, dx) + core,
                    ).start()
                else:
                    pltpu.make_async_copy(shifted.at[which], slot, grad_recv.at[which]).start()

        def arrive(which):
            wait_all(grad_full.at[token_rows(which)], grad_recv.at[which])

        def deliver(which, product):
            parts_even[which * count:(which + 1) * count] = product.reshape(
                count, shard, quarter
            ).astype(BF16)
            slot = got_even.at[(2 * mine + core) * chips + chip]
            target = base + which
            for dy, dx in offsets:
                for swap in (1, 0):
                    lane = 2 * chip_at(dy, dx) + (1 - core if swap else core)
                    copy = remote(
                        parts_even.at[which * count + lane], slot, dx_send, dx_recv.at[0], target, lane
                    )
                    if dy or dx or swap:
                        copy.start()
                    else:
                        pl.when(mine != which)(copy.start)

        gradient_phase(chosen, arrive, deliver)
        pltpu.make_async_copy(
            parts_even.at[mine * count + tensor],
            got_even.at[(2 * mine + core) * chips + chip],
            dx_recv.at[0],
        ).start()
        weight_phase()
        hand_over().wait_recv()
        wait_all(got_even, dx_recv.at[0])
        for place in range(4):
            total = got_even[place * chips].astype(F32)
            for slot in range(1, chips):
                total = total + got_even[place * chips + slot].astype(F32)
            part = quarter_columns(place)
            dx_own[:, part] = (grad_own[:, part].astype(F32) + total).astype(BF16)
        store_dx.start()
        wait_all(grad_full.at[pl.ds(0, 2 * (chips - 1) * block)], grad_send)
        wait_all(got_even.at[pl.ds(0, 2 * count - 1)], dx_send)

    pl.when(odd == 1)(odd_section)
    pl.when(odd == 0)(even_section)
    gather_sent(x_in, x_send)
    for copy in (send_version, send_probs, send_wo, send_wv):
        copy.wait_send()
    x_chain[4]()
    grad_chain[4]()
    for copy in (send_gv, send_go):
        copy.wait()
    for copy in (store_dx, store_gv, store_go):
        copy.wait()


def on_device(section_input, query, key_stash, incoming, version, w_value, w_out):
    count = lax.axis_size("tensor")
    shard, width = section_input.shape[1:]
    rows, tokens = query.shape[1:]
    half = width // 2
    quarter = half // 2
    heads = rows // HEAD_DIM
    anywhere = pl.BlockSpec(memory_space=pl.ANY)
    weight = pltpu.VMEM((2, 2 * rows, quarter), BF16)
    blocks = pltpu.VMEM((2 * count, shard, quarter), BF16)
    big_blocks = pltpu.VMEM((count, 2 * shard, quarter), BF16)
    full = pltpu.VMEM((2 * tokens, quarter), BF16)
    pair = pltpu.VMEM((2, rows, tokens), BF16)
    chain = [
        pltpu.VMEM((2, 2 * rows, tokens), F32),
        pltpu.VMEM((2, 2 * rows, tokens), BF16),
        pair,
        pltpu.VMEM((2, rows, tokens), F32),
        pair,
        pair,
        pltpu.VMEM((2 * rows, 2 * tokens), BF16),
    ]
    own = pltpu.VMEM((shard, width), BF16)
    result = pltpu.VMEM((rows, quarter), BF16)
    two = pltpu.VMEM((2, 2 * shard, quarter), BF16)
    dma = pltpu.SemaphoreType.DMA
    return pl.pallas_call(
        functools.partial(kernel, count),
        out_shape=(
            jax.ShapeDtypeStruct((1, shard, width), BF16),
            jax.ShapeDtypeStruct((1, rows, half), BF16),
            jax.ShapeDtypeStruct((1, rows, half), BF16),
        ),
        in_specs=[anywhere] * 4 + [pl.BlockSpec(memory_space=pltpu.SMEM)] + [anywhere] * 2,
        out_specs=(anywhere, anywhere, anywhere),
        scratch_shapes=[
            weight, weight,
            pltpu.VMEM((rows, tokens), BF16),
            pltpu.VMEM((rows, tokens), BF16),
            pltpu.VMEM((2, heads, tokens, tokens), BF16),
            pltpu.VMEM((2, 8, 128), jnp.int32),
            blocks, blocks, full, full,
            *chain, *chain,
            full, big_blocks, blocks, blocks,
            two, two,
            pltpu.VMEM((2, 2, shard, quarter), BF16),
            pltpu.VMEM((4, shard, quarter), BF16),
            own, own, result, result, result, result,
            dma((4,)), dma((6,)), dma((6,)), dma((12,)), dma((12,)),
            dma, dma((2,)), dma, dma((2,)), dma, dma((2,)),
            dma((2,)), dma((2,)), dma, dma, dma, dma, dma((3,)),
        ],
        compiler_params=pltpu.CompilerParams(
            collective_id=0, has_side_effects=True, vmem_limit_bytes=60 * 1024 * 1024
        ),
    )(section_input, query, key_stash, incoming, version, w_value, w_out)


def solution(mesh):
    split = P("section", "tensor", None)
    weights = P("section", None, "tensor", None)
    return jax.shard_map(
        on_device,
        mesh=mesh,
        in_specs=(split, split, split, split, P("section"), weights, weights),
        out_specs=(split, split, split),
        check_vma=False,
    )
```

```python
import functools
import math

import jax
import jax.numpy as jnp
from jax import lax
from jax.experimental import pallas as pl
from jax.experimental.pallas import tpu as pltpu
from jax.sharding import PartitionSpec as P

HEAD_DIM = 96
BF16 = jnp.bfloat16
F32 = jnp.float32
MESH = pl.DeviceIdType.MESH


def dot(left, right, left_dim, right_dim):
    return lax.dot_general(
        left, right, (((left_dim,), (right_dim,)), ((), ())), preferred_element_type=F32
    )


def kernel(
    count,
    x_ref, query_ref, key_ref, incoming_ref, version_ref, wv_ref, wo_ref,
    dx_ref, gv_ref, go_ref,
    wv, wo, query, key, probs, versions,
    x_in, grad_in, x_full, grad_full,
    part_x, cast_x, sib_x, total_x, sent_x, got_x, context,
    part_g, cast_g, sib_g, total_g, sent_g, got_g, value_grad,
    parts_odd, got_odd, parts_even, got_even,
    reduced, shifted, pieces, assembled, grad_own, gv_sent, go_sent,
    load_sem, pair_send, pair_recv, sib_send, sib_recv,
    x_send, x_recv, grad_send, grad_recv, dx_send, dx_recv,
    shift_send, shift_recv, piece_send, piece_recv, own_send, own_recv,
):
    section = lax.axis_index("section")
    tensor = lax.axis_index("tensor")
    mine = lax.rem(section, 2)
    base = section - mine
    partner = base + 1 - mine
    odd = lax.rem(section // 2, 2)
    other = section + 2 - 4 * odd
    core = lax.rem(tensor, 2)
    chip = tensor // 2
    sibling = tensor + 1 - 2 * core
    rows = wv.shape[1] // 2
    quarter = wv.shape[2]
    half = 2 * quarter
    heads = rows // HEAD_DIM
    shard = grad_own.shape[0]
    tokens = count * shard
    chips = count // 2
    block = 2 * shard
    own_rows = pl.ds(pl.multiple_of(core * rows, 16), rows)
    sib_rows = pl.ds(pl.multiple_of((1 - core) * rows, 16), rows)

    offsets = [(dy, dx) for dx in (1, 0) for dy in sorted(range(chips // 2), key=lambda d: (-min(d, chips // 2 - d), d))]

    def chip_at(dy, dx):
        side = lax.rem(chip, 2)
        return 2 * lax.rem(chip // 2 + dy, chips // 2) + (1 - side if dx else side)

    def columns(side, which):
        return pl.ds(pl.multiple_of(side * half + which * quarter, 128), quarter)

    def remote(source, destination, send, recv, target, lane):
        return pltpu.make_async_remote_copy(
            src_ref=source,
            dst_ref=destination,
            send_sem=send,
            recv_sem=recv,
            device_id=(target, lane),
            device_id_type=MESH,
        )

    def to_partner(source, destination, index):
        return remote(
            source, destination, pair_send.at[index], pair_recv.at[index], partner, tensor
        )

    def to_sibling(source, destination, index):
        return remote(
            source, destination, sib_send.at[index], sib_recv.at[index], section, sibling
        )

    def wait_all(buffer, sem):
        pltpu.make_async_copy(buffer, buffer, sem).wait()

    loads = [
        pltpu.make_async_copy(query_ref.at[0], query, load_sem.at[0]),
        pltpu.make_async_copy(key_ref.at[0], key, load_sem.at[1]),
        pltpu.make_async_copy(
            wo_ref.at[0, :, :, columns(0, core)], wo.at[:, own_rows], load_sem.at[2]
        ),
        pltpu.make_async_copy(
            wv_ref.at[0, :, :, columns(0, core)], wv.at[:, own_rows], load_sem.at[3]
        ),
    ]
    for load in loads:
        load.start()
    versions[mine] = jnp.full(versions.shape[1:], version_ref[0], jnp.int32)

    barrier = pltpu.get_barrier_semaphore()

    def signal(target, lane):
        pl.semaphore_signal(barrier, inc=1, device_id=(target, lane), device_id_type=MESH)

    def greet(target, first):
        def step(j, carry):
            signal(target, lax.rem(tensor + j, count))
            return carry

        lax.fori_loop(first, count, step, 0)

    signal(other, tensor)
    greet(partner, 0)
    greet(section, 1)
    pl.semaphore_wait(barrier, 2 * count)

    send_version = to_partner(versions.at[mine], versions.at[mine], 0)
    send_probs = to_partner(probs.at[mine], probs.at[mine], 1)
    send_wo = to_sibling(wo_ref.at[0, :, :, columns(0, 1 - core)], wo.at[:, own_rows], 0)
    send_wv = to_sibling(wv_ref.at[0, :, :, columns(0, 1 - core)], wv.at[:, own_rows], 1)

    def gather_start(source, buffer, send, recv):
        slot = buffer.at[mine * count + tensor]
        for dy, dx in offsets:
            for swap in (1, 0):
                lane_core = 1 - core if swap else core
                lane = 2 * chip_at(dy, dx) + lane_core
                remote(
                    source.at[:, columns(1 - mine, lane_core)], slot, send, recv.at[mine], partner, lane
                ).start()
        for dy, dx in offsets:
            for swap in (1, 0):
                if dy or dx or swap:
                    lane_core = 1 - core if swap else core
                    lane = 2 * chip_at(dy, dx) + lane_core
                    remote(
                        source.at[:, columns(mine, lane_core)], slot, send, recv.at[mine], section, lane
                    ).start()
        pltpu.make_async_copy(source.at[:, columns(mine, core)], slot, recv.at[mine]).start()

    def gather_wait(buffer, full, recv, which):
        wait_all(buffer.at[pl.ds(which * count, count)], recv.at[which])

        def step(i, carry):
            pair = buffer[pl.ds(which * count + 2 * i, 2)].astype(F32).reshape(block, quarter)
            start = pl.multiple_of(which * tokens + i * block, block)
            full[pl.ds(start, block), :] = pair.astype(BF16)
            return carry

        lax.fori_loop(0, chips, step, 0, unroll=True)

    def gather_sent(buffer, send):
        wait_all(buffer.at[pl.ds(0, 2 * count - 1)], send)

    def attention():
        send_version.start()
        send_wo.start()
        send_wv.start()
        loads[0].wait()
        loads[1].wait()
        row = lax.broadcasted_iota(jnp.int32, (tokens, tokens), 0)
        causal = lax.broadcasted_iota(jnp.int32, (tokens, tokens), 1) <= row
        for head in range(heads):
            part = slice(head * HEAD_DIM, (head + 1) * HEAD_DIM)
            scores = dot(query[part], key[part], 0, 0) * (1.0 / math.sqrt(HEAD_DIM))
            scores = jnp.where(causal, scores, -jnp.inf)
            expo = jnp.exp(scores - jnp.max(scores, axis=1, keepdims=True))
            attend = expo / jnp.sum(expo, axis=1, keepdims=True)
            probs[mine, head] = attend.astype(BF16)
        send_probs.start()
        for load in loads[2:]:
            load.wait()
        send_wo.wait_recv()
        send_wv.wait_recv()
        send_version.wait_recv()
        return [jnp.max(versions[which]) for which in range(2)]

    def token_rows(which):
        return slice(which * tokens, (which + 1) * tokens)

    def chain(weight, full, part, cast, sib, total, sent, got, out, side, first_sib, first_pair):
        def first_copy(which):
            return to_sibling(cast.at[which, sib_rows], sib.at[which], first_sib + which)

        def second_copy(which):
            return to_partner(sent.at[which], got.at[which], first_pair + which)

        def third_copy(which):
            place = out.at[own_rows, token_rows(which)]
            return to_sibling(place, place, first_sib + 2 + which)

        def first(which, version):
            product = dot(weight[version], full[token_rows(which)], 1, 1)
            part[which] = product
            cast[which] = product.astype(BF16)
            first_copy(which).start()

        def second(which):
            first_copy(which).wait_recv()
            chip_sum = part[which, own_rows] + sib[which].astype(F32)
            total[which] = chip_sum
            sent[which] = chip_sum.astype(BF16)
            second_copy(which).start()

        def third(which):
            second_copy(which).wait_recv()
            for head in range(heads):
                block_rows = slice(head * HEAD_DIM, (head + 1) * HEAD_DIM)
                whole = total[which, block_rows] + got[which, block_rows].astype(F32)
                mixed = dot(whole.astype(BF16), probs[which, head], 1, side)
                start = pl.multiple_of(core * rows + head * HEAD_DIM, 16)
                out[pl.ds(start, HEAD_DIM), token_rows(which)] = mixed.astype(BF16)
            third_copy(which).start()

        def last(which):
            third_copy(which).wait_recv()

        def sent_wait():
            for which in range(2):
                first_copy(which).wait_send()
                second_copy(which).wait_send()
                third_copy(which).wait_send()

        return first, second, third, last, sent_wait

    x_chain = chain(
        wv, x_full, part_x, cast_x, sib_x, total_x, sent_x, got_x, context, 1, 2, 2
    )
    grad_chain = chain(
        wo, grad_full, part_g, cast_g, sib_g, total_g, sent_g, got_g, value_grad, 0, 6, 4
    )

    def context_phase(chosen, before_third=lambda: None):
        first, second, third, last, _ = x_chain
        for which in range(2):
            gather_wait(x_in, x_full, x_recv, which)
            first(which, chosen[which])
        for which in range(2):
            second(which)
        before_third()
        for which in range(2):
            third(which)
        for which in range(2):
            last(which)

    def gradient_phase(chosen, arrive, deliver, before_third=lambda: None):
        first, second, third, last, _ = grad_chain
        for which in range(2):
            arrive(which)
            first(which, chosen[which])
        for which in range(2):
            second(which)
        before_third()
        for which in range(2):
            third(which)
        for which in range(2):
            last(which)
            deliver(
                which, dot(value_grad[:, token_rows(which)], wv[chosen[which]], 0, 0)
            )

    send_gv = to_sibling(gv_sent, gv_ref.at[0, :, columns(0, core)], 10)
    send_go = to_sibling(go_sent, go_ref.at[0, :, columns(0, core)], 11)

    def weight_phase():
        for terms, full, kept, sent, send in (
            (value_grad, x_full, gv_ref, gv_sent, send_gv),
            (context, grad_full, go_ref, go_sent, send_go),
        ):
            sent[...] = dot(terms[sib_rows], full[...], 1, 0).astype(BF16)
            send.start()
            kept[0, :, columns(0, core)] = dot(terms[own_rows], full[...], 1, 0).astype(BF16)

    def chip_rows(which, place):
        return pl.ds(pl.multiple_of(which * tokens + place * block, block), block)

    def shift(which):
        return remote(
            reduced.at[which], shifted.at[which],
            shift_send.at[which], shift_recv.at[which], other, tensor,
        )

    def hand_over():
        return remote(dx_ref.at[0], grad_own, own_send, own_recv, other, tensor)

    def quarter_columns(place):
        return slice(place * quarter, (place + 1) * quarter)

    def odd_section():
        gather_start(incoming_ref.at[0], grad_in, grad_send, grad_recv)
        chosen = attention()

        def arrive(which):
            gather_wait(grad_in, grad_full, grad_recv, which)

        def deliver(which, product):
            parts_odd[token_rows(which)] = product.astype(BF16)
            slot = got_odd.at[which * chips + chip]
            for dy, dx in offsets:
                place = chip_at(dy, dx)
                source = parts_odd.at[chip_rows(which, place)]
                if dy or dx:
                    remote(
                        source, slot, dx_send, dx_recv.at[which], section, 2 * place + core
                    ).start()
                else:
                    pltpu.make_async_copy(source, slot, dx_recv.at[which]).start()

        gradient_phase(chosen, arrive, deliver, send_probs.wait_recv)
        for which in range(2):
            wait_all(got_odd.at[pl.ds(which * chips, chips)], dx_recv.at[which])
            total = got_odd[which * chips].astype(F32)
            for place in range(1, chips):
                total = total + got_odd[which * chips + place].astype(F32)
            total = total + grad_full[chip_rows(which, chip), :].astype(F32)
            result = total.astype(BF16)
            reduced[which] = result
            shift(which).start()
            pieces[which] = total.reshape(2, shard, quarter).astype(BF16)
        gather_start(x_ref.at[0], x_in, x_send, x_recv)
        slot = assembled.at[2 * mine + core]
        pltpu.make_async_copy(pieces.at[mine, core], slot, piece_recv).start()
        for target, line, lane, lane_core in (
            (section, mine, sibling, 1 - core),
            (partner, 1 - mine, tensor, core),
            (partner, 1 - mine, sibling, 1 - core),
        ):
            remote(pieces.at[line, lane_core], slot, piece_send, piece_recv, target, lane).start()
        wait_all(assembled, piece_recv)
        for place in range(4):
            dx_ref[0, :, quarter_columns(place)] = assembled[place]
        hand_over().start()
        context_phase(chosen)
        weight_phase()
        gather_sent(grad_in, grad_send)
        wait_all(got_odd.at[pl.ds(0, 2 * chips - 2)], dx_send)
        for which in range(2):
            shift(which).wait_send()
        wait_all(assembled.at[pl.ds(0, 3)], piece_send)
        hand_over().wait_send()

    def even_section():
        gather_start(x_ref.at[0], x_in, x_send, x_recv)
        chosen = attention()
        context_phase(chosen, send_probs.wait_recv)
        for which in range(2):
            shift(which).wait_recv()
            slot = grad_full.at[chip_rows(which, chip)]
            for dy, dx in offsets:
                if dy or dx:
                    remote(
                        shifted.at[which], slot, grad_send, grad_recv.at[which],
                        section, 2 * chip_at(dy, dx) + core,
                    ).start()
                else:
                    pltpu.make_async_copy(shifted.at[which], slot, grad_recv.at[which]).start()

        def arrive(which):
            wait_all(grad_full.at[token_rows(which)], grad_recv.at[which])

        def deliver(which, product):
            parts_even[which * count:(which + 1) * count] = product.reshape(
                count, shard, quarter
            ).astype(BF16)
            slot = got_even.at[(2 * mine + core) * chips + chip]
            target = base + which
            for dy, dx in offsets:
                for swap in (1, 0):
                    lane = 2 * chip_at(dy, dx) + (1 - core if swap else core)
                    copy = remote(
                        parts_even.at[which * count + lane], slot, dx_send, dx_recv.at[0], target, lane
                    )
                    if dy or dx or swap:
                        copy.start()
                    else:
                        pl.when(mine != which)(copy.start)

        gradient_phase(chosen, arrive, deliver)
        pltpu.make_async_copy(
            parts_even.at[mine * count + tensor],
            got_even.at[(2 * mine + core) * chips + chip],
            dx_recv.at[0],
        ).start()
        weight_phase()
        hand_over().wait_recv()
        wait_all(got_even, dx_recv.at[0])
        for place in range(4):
            total = got_even[place * chips].astype(F32)
            for slot in range(1, chips):
                total = total + got_even[place * chips + slot].astype(F32)
            part = quarter_columns(place)
            dx_ref[0, :, part] = (grad_own[:, part].astype(F32) + total).astype(BF16)
        wait_all(grad_full.at[pl.ds(0, 2 * (chips - 1) * block)], grad_send)
        wait_all(got_even.at[pl.ds(0, 2 * count - 1)], dx_send)

    pl.when(odd == 1)(odd_section)
    pl.when(odd == 0)(even_section)
    gather_sent(x_in, x_send)
    for copy in (send_version, send_probs, send_wo, send_wv):
        copy.wait_send()
    x_chain[4]()
    grad_chain[4]()
    for copy in (send_gv, send_go):
        copy.wait()


def store_kernel(dx, gv, go, dx_out, gv_out, go_out, sem):
    copies = [
        pltpu.make_async_copy(source, result, sem.at[index])
        for index, (source, result) in enumerate(((dx, dx_out), (gv, gv_out), (go, go_out)))
    ]
    for copy in copies:
        copy.start()
    for copy in copies:
        copy.wait()


def on_device(section_input, query, key_stash, incoming, version, w_value, w_out):
    count = lax.axis_size("tensor")
    shard, width = section_input.shape[1:]
    rows, tokens = query.shape[1:]
    half = width // 2
    quarter = half // 2
    heads = rows // HEAD_DIM
    hbm = pl.BlockSpec(memory_space=pltpu.HBM)
    local = pl.BlockSpec(memory_space=pltpu.VMEM)
    weight = pltpu.VMEM((2, 2 * rows, quarter), BF16)
    blocks = pltpu.VMEM((2 * count, shard, quarter), BF16)
    big_blocks = pltpu.VMEM((count, 2 * shard, quarter), BF16)
    full = pltpu.VMEM((2 * tokens, quarter), BF16)
    pair = pltpu.VMEM((2, rows, tokens), BF16)
    chain = [
        pltpu.VMEM((2, 2 * rows, tokens), F32),
        pltpu.VMEM((2, 2 * rows, tokens), BF16),
        pair,
        pltpu.VMEM((2, rows, tokens), F32),
        pair,
        pair,
        pltpu.VMEM((2 * rows, 2 * tokens), BF16),
    ]
    own = pltpu.VMEM((shard, width), BF16)
    result = pltpu.VMEM((rows, quarter), BF16)
    two = pltpu.VMEM((2, 2 * shard, quarter), BF16)
    dma = pltpu.SemaphoreType.DMA
    shapes = ((1, shard, width), (1, rows, half), (1, rows, half))
    results = pl.pallas_call(
        functools.partial(kernel, count),
        out_shape=tuple(pltpu.VMEM(shape, BF16) for shape in shapes),
        in_specs=[hbm] * 4 + [pl.BlockSpec(memory_space=pltpu.SMEM)] + [hbm] * 2,
        out_specs=(local, local, local),
        scratch_shapes=[
            weight, weight,
            pltpu.VMEM((rows, tokens), BF16),
            pltpu.VMEM((rows, tokens), BF16),
            pltpu.VMEM((2, heads, tokens, tokens), BF16),
            pltpu.VMEM((2, 8, 128), jnp.int32),
            blocks, blocks, full, full,
            *chain, *chain,
            full, big_blocks, blocks, blocks,
            two, two,
            pltpu.VMEM((2, 2, shard, quarter), BF16),
            pltpu.VMEM((4, shard, quarter), BF16),
            own, result, result,
            dma((4,)), dma((6,)), dma((6,)), dma((12,)), dma((12,)),
            dma, dma((2,)), dma, dma((2,)), dma, dma((2,)),
            dma((2,)), dma((2,)), dma, dma, dma, dma,
        ],
        compiler_params=pltpu.CompilerParams(
            collective_id=0, has_side_effects=True, vmem_limit_bytes=56 * 1024 * 1024
        ),
    )(section_input, query, key_stash, incoming, version, w_value, w_out)
    return pl.pallas_call(
        store_kernel,
        out_shape=tuple(jax.ShapeDtypeStruct(shape, BF16) for shape in shapes),
        in_specs=[local] * 3,
        out_specs=(hbm, hbm, hbm),
        scratch_shapes=[dma((3,))],
        compiler_params=pltpu.CompilerParams(vmem_limit_bytes=4 * 1024 * 1024),
    )(*results)


def solution(mesh):
    split = P("section", "tensor", None)
    weights = P("section", None, "tensor", None)
    return jax.shard_map(
        on_device,
        mesh=mesh,
        in_specs=(split, split, split, split, P("section"), weights, weights),
        out_specs=(split, split, split),
        check_vma=False,
    )
```

```python
import functools
import math

import jax
import jax.numpy as jnp
from jax import lax
from jax.experimental import pallas as pl
from jax.experimental.pallas import tpu as pltpu
from jax.sharding import PartitionSpec as P

HEAD_DIM = 96
CUTS = 2
BF16 = jnp.bfloat16
F32 = jnp.float32
MESH = pl.DeviceIdType.MESH


def dot(left, right, left_dim, right_dim):
    return lax.dot_general(
        left, right, (((left_dim,), (right_dim,)), ((), ())), preferred_element_type=F32
    )


def kernel(
    count,
    x_ref, query_ref, key_ref, incoming_ref, version_ref, wv_ref, wo_ref,
    dx_ref, gv_ref, go_ref,
    wv, wo, query, key, probs, versions,
    x_in, grad_in, x_full, grad_full,
    part_x, cast_x, sib_x, total_x, sent_x, got_x, context,
    part_g, cast_g, sib_g, total_g, sent_g, got_g, value_grad,
    parts_odd, got_odd, parts_even, got_even,
    reduced, shifted, pieces, assembled, row, grad_own, gv_sent, go_sent,
    load_sem, pair_send, pair_recv, sib_send, sib_recv,
    x_send, x_recv, grad_send, grad_recv, dx_send, dx_recv,
    shift_send, shift_recv, piece_send, piece_recv, own_send, own_recv,
):
    section = lax.axis_index("section")
    tensor = lax.axis_index("tensor")
    mine = lax.rem(section, 2)
    base = section - mine
    partner = base + 1 - mine
    odd = lax.rem(section // 2, 2)
    other = section + 2 - 4 * odd
    core = lax.rem(tensor, 2)
    chip = tensor // 2
    sibling = tensor + 1 - 2 * core
    rows = wv.shape[1] // 2
    quarter = wv.shape[2]
    half = 2 * quarter
    heads = rows // HEAD_DIM
    shard = grad_own.shape[0]
    tokens = count * shard
    chips = count // 2
    block = 2 * shard
    own_rows = pl.ds(pl.multiple_of(core * rows, 16), rows)
    sib_rows = pl.ds(pl.multiple_of((1 - core) * rows, 16), rows)

    offsets = [(dy, dx) for dx in (1, 0) for dy in sorted(range(chips // 2), key=lambda d: (-min(d, chips // 2 - d), d))]

    def chip_at(dy, dx):
        side = lax.rem(chip, 2)
        return 2 * lax.rem(chip // 2 + dy, chips // 2) + (1 - side if dx else side)

    def columns(side, which):
        return pl.ds(pl.multiple_of(side * half + which * quarter, 128), quarter)

    def remote(source, destination, send, recv, target, lane):
        return pltpu.make_async_remote_copy(
            src_ref=source,
            dst_ref=destination,
            send_sem=send,
            recv_sem=recv,
            device_id=(target, lane),
            device_id_type=MESH,
        )

    def to_partner(source, destination, index):
        return remote(
            source, destination, pair_send.at[index], pair_recv.at[index], partner, tensor
        )

    def to_sibling(source, destination, index):
        return remote(
            source, destination, sib_send.at[index], sib_recv.at[index], section, sibling
        )

    def wait_all(buffer, sem):
        pltpu.make_async_copy(buffer, buffer, sem).wait()

    loads = [
        pltpu.make_async_copy(query_ref.at[0], query, load_sem.at[0]),
        pltpu.make_async_copy(key_ref.at[0], key, load_sem.at[1]),
        pltpu.make_async_copy(
            wo_ref.at[0, :, :, columns(0, core)], wo.at[:, own_rows], load_sem.at[2]
        ),
        pltpu.make_async_copy(
            wv_ref.at[0, :, :, columns(0, core)], wv.at[:, own_rows], load_sem.at[3]
        ),
    ]
    load_incoming = pltpu.make_async_copy(incoming_ref.at[0], row, load_sem.at[4])
    load_x = pltpu.make_async_copy(x_ref.at[0], row, load_sem.at[4])
    pl.when(odd == 1)(load_incoming.start)
    pl.when(odd == 0)(load_x.start)
    for load in loads:
        load.start()
    versions[mine] = jnp.full(versions.shape[1:], version_ref[0], jnp.int32)

    barrier = pltpu.get_barrier_semaphore()

    def signal(target, lane):
        pl.semaphore_signal(barrier, inc=1, device_id=(target, lane), device_id_type=MESH)

    for dy, dx in offsets:
        place = chip_at(dy, dx)
        for swap in (1, 0):
            lane = 2 * place + (1 - core if swap else core)
            signal(partner, lane)
            if dy or dx or swap:
                signal(section, lane)
    signal(other, tensor)
    pl.semaphore_wait(barrier, 2 * count)

    send_version = to_partner(versions.at[mine], versions.at[mine], 0)
    send_probs = to_partner(probs.at[mine], probs.at[mine], 1)
    send_wo = to_sibling(wo_ref.at[0, :, :, columns(0, 1 - core)], wo.at[:, own_rows], 0)
    send_wv = to_sibling(wv_ref.at[0, :, :, columns(0, 1 - core)], wv.at[:, own_rows], 1)

    def gather_start(source, buffer, send, recv):
        slot = buffer.at[mine * count + tensor]
        for dy, dx in offsets:
            for swap in (1, 0):
                lane_core = 1 - core if swap else core
                lane = 2 * chip_at(dy, dx) + lane_core
                remote(
                    source.at[:, columns(1 - mine, lane_core)], slot, send, recv.at[mine], partner, lane
                ).start()
        for dy, dx in offsets:
            for swap in (1, 0):
                if dy or dx or swap:
                    lane_core = 1 - core if swap else core
                    lane = 2 * chip_at(dy, dx) + lane_core
                    remote(
                        source.at[:, columns(mine, lane_core)], slot, send, recv.at[mine], section, lane
                    ).start()
        pltpu.make_async_copy(source.at[:, columns(mine, core)], slot, recv.at[mine]).start()

    def gather_wait(buffer, full, recv, which):
        wait_all(buffer.at[pl.ds(which * count, count)], recv.at[which])

        def step(i, carry):
            pair = buffer[pl.ds(which * count + 2 * i, 2)].astype(F32).reshape(block, quarter)
            start = pl.multiple_of(which * tokens + i * block, block)
            full[pl.ds(start, block), :] = pair.astype(BF16)
            return carry

        lax.fori_loop(0, chips, step, 0, unroll=True)

    def gather_sent(buffer, send):
        wait_all(buffer.at[pl.ds(0, 2 * count - 1)], send)

    def attention():
        send_version.start()
        send_wo.start()
        send_wv.start()
        loads[0].wait()
        loads[1].wait()
        line = lax.broadcasted_iota(jnp.int32, (tokens, tokens), 0)
        causal = lax.broadcasted_iota(jnp.int32, (tokens, tokens), 1) <= line
        for head in range(heads):
            part = slice(head * HEAD_DIM, (head + 1) * HEAD_DIM)
            scores = dot(query[part], key[part], 0, 0) * (1.0 / math.sqrt(HEAD_DIM))
            scores = jnp.where(causal, scores, -jnp.inf)
            expo = jnp.exp(scores - jnp.max(scores, axis=1, keepdims=True))
            attend = expo / jnp.sum(expo, axis=1, keepdims=True)
            probs[mine, head] = attend.astype(BF16)
        send_probs.start()
        for load in loads[2:]:
            load.wait()
        send_wo.wait_recv()
        send_wv.wait_recv()
        send_version.wait_recv()
        return [jnp.max(versions[which]) for which in range(2)]

    def token_rows(which):
        return slice(which * tokens, (which + 1) * tokens)

    def chain(weight, full, part, cast, sib, total, sent, got, out, side, first_sib, first_pair):
        def first_copy(which):
            return to_sibling(cast.at[which, sib_rows], sib.at[which], first_sib + which)

        def second_copy(which):
            return to_partner(sent.at[which], got.at[which], first_pair + which)

        def third_copy(which):
            place = out.at[own_rows, token_rows(which)]
            return to_sibling(place, place, first_sib + 2 + which)

        def first(which, version):
            product = dot(weight[version], full[token_rows(which)], 1, 1)
            part[which] = product
            cast[which] = product.astype(BF16)
            first_copy(which).start()

        def second(which):
            first_copy(which).wait_recv()
            chip_sum = part[which, own_rows] + sib[which].astype(F32)
            total[which] = chip_sum
            sent[which] = chip_sum.astype(BF16)
            second_copy(which).start()

        def third(which):
            second_copy(which).wait_recv()
            for head in range(heads):
                block_rows = slice(head * HEAD_DIM, (head + 1) * HEAD_DIM)
                whole = total[which, block_rows] + got[which, block_rows].astype(F32)
                mixed = dot(whole.astype(BF16), probs[which, head], 1, side)
                start = pl.multiple_of(core * rows + head * HEAD_DIM, 16)
                out[pl.ds(start, HEAD_DIM), token_rows(which)] = mixed.astype(BF16)
            third_copy(which).start()

        def last(which):
            third_copy(which).wait_recv()

        def sent_wait():
            for which in range(2):
                first_copy(which).wait_send()
                second_copy(which).wait_send()
                third_copy(which).wait_send()

        return first, second, third, last, sent_wait

    x_chain = chain(
        wv, x_full, part_x, cast_x, sib_x, total_x, sent_x, got_x, context, 1, 2, 2
    )
    grad_chain = chain(
        wo, grad_full, part_g, cast_g, sib_g, total_g, sent_g, got_g, value_grad, 0, 6, 4
    )

    def context_phase(chosen, before_third=lambda: None):
        first, second, third, last, _ = x_chain
        for which in range(2):
            gather_wait(x_in, x_full, x_recv, which)
            first(which, chosen[which])
        for which in range(2):
            second(which)
        before_third()
        for which in range(2):
            third(which)
        for which in range(2):
            last(which)

    def gradient_phase(chosen, arrive, deliver, before_third=lambda: None):
        first, second, third, last, _ = grad_chain
        def last_step(which):
            last(which)
            weight = wv.at[chosen[which]]
            deliver(
                which, lambda part: dot(value_grad[:, token_rows(which)], weight[:, part], 0, 0)
            )

        arrive(0)
        first(0, chosen[0])
        second(0)
        arrive(1)
        first(1, chosen[1])
        second(1)
        before_third()
        third(0)
        last_step(0)
        third(1)
        last_step(1)

    send_gv = to_sibling(gv_sent, gv_ref.at[0, :, columns(0, core)], 10)
    send_go = to_sibling(go_sent, go_ref.at[0, :, columns(0, core)], 11)

    def weight_phase():
        for terms, full, kept, sent, send in (
            (value_grad, x_full, gv_ref, gv_sent, send_gv),
            (context, grad_full, go_ref, go_sent, send_go),
        ):
            sent[...] = dot(terms[sib_rows], full[...], 1, 0).astype(BF16)
            send.start()
            kept[0, :, columns(0, core)] = dot(terms[own_rows], full[...], 1, 0).astype(BF16)

    def chip_rows(which, place):
        return pl.ds(pl.multiple_of(which * tokens + place * block, block), block)

    def cut_columns(cut):
        return slice(cut * (quarter // CUTS), (cut + 1) * (quarter // CUTS))

    all_cuts = [(which, cut) for which in range(2) for cut in range(CUTS)]

    def shift(which, cut):
        place = which * CUTS + cut
        return remote(
            reduced.at[which, :, cut_columns(cut)], shifted.at[which, :, cut_columns(cut)],
            shift_send.at[place], shift_recv.at[place], other, tensor,
        )

    def hand_over():
        return remote(dx_ref.at[0], grad_own, own_send, own_recv, other, tensor)

    def quarter_columns(place):
        return slice(place * quarter, (place + 1) * quarter)

    def odd_section():
        load_incoming.wait()
        gather_start(row, grad_in, grad_send, grad_recv)
        chosen = attention()

        def arrive(which):
            gather_wait(grad_in, grad_full, grad_recv, which)

        def deliver(which, multiply):
            for cut in range(CUTS):
                parts_odd[token_rows(which), cut_columns(cut)] = multiply(cut_columns(cut)).astype(BF16)
                slot = got_odd.at[which * chips + chip, :, cut_columns(cut)]
                arrived = dx_recv.at[which * CUTS + cut]
                for dy, dx in offsets:
                    place = chip_at(dy, dx)
                    source = parts_odd.at[chip_rows(which, place), cut_columns(cut)]
                    if dy or dx:
                        remote(source, slot, dx_send, arrived, section, 2 * place + core).start()
                    else:
                        pltpu.make_async_copy(source, slot, arrived).start()

        gradient_phase(chosen, arrive, deliver, send_probs.wait_recv)
        for which, cut in all_cuts:
            part = cut_columns(cut)
            wait_all(
                got_odd.at[pl.ds(which * chips, chips), :, part], dx_recv.at[which * CUTS + cut]
            )
            total = got_odd[which * chips, :, part].astype(F32)
            for place in range(1, chips):
                total = total + got_odd[which * chips + place, :, part].astype(F32)
            total = total + grad_full[chip_rows(which, chip), part].astype(F32)
            reduced[which, :, part] = total.astype(BF16)
            shift(which, cut).start()
            pieces[which, :, :, part] = total.reshape(2, shard, quarter // CUTS).astype(BF16)
        gather_start(x_ref.at[0], x_in, x_send, x_recv)
        slot = assembled.at[2 * mine + core]
        pltpu.make_async_copy(pieces.at[mine, core], slot, piece_recv).start()
        for target, line, lane, lane_core in (
            (section, mine, sibling, 1 - core),
            (partner, 1 - mine, tensor, core),
            (partner, 1 - mine, sibling, 1 - core),
        ):
            remote(pieces.at[line, lane_core], slot, piece_send, piece_recv, target, lane).start()
        wait_all(assembled, piece_recv)
        for place in range(4):
            dx_ref[0, :, quarter_columns(place)] = assembled[place]
        hand_over().start()
        context_phase(chosen)
        weight_phase()
        gather_sent(grad_in, grad_send)
        wait_all(got_odd.at[pl.ds(0, 2 * chips - 2)], dx_send)
        for which, cut in all_cuts:
            shift(which, cut).wait_send()
        wait_all(assembled.at[pl.ds(0, 3)], piece_send)
        hand_over().wait_send()

    def even_section():
        load_x.wait()
        gather_start(row, x_in, x_send, x_recv)
        chosen = attention()
        context_phase(chosen, send_probs.wait_recv)
        for which, cut in all_cuts:
            shift(which, cut).wait_recv()
            source = shifted.at[which, :, cut_columns(cut)]
            slot = grad_full.at[chip_rows(which, chip), cut_columns(cut)]
            for dy, dx in offsets:
                if dy or dx:
                    remote(
                        source, slot, grad_send, grad_recv.at[which],
                        section, 2 * chip_at(dy, dx) + core,
                    ).start()
                else:
                    pltpu.make_async_copy(source, slot, grad_recv.at[which]).start()

        def arrive(which):
            wait_all(grad_full.at[token_rows(which)], grad_recv.at[which])

        def deliver(which, multiply):
            product = multiply(slice(None))
            parts_even[which * count:(which + 1) * count] = product.reshape(
                count, shard, quarter
            ).astype(BF16)
            slot = got_even.at[(2 * mine + core) * chips + chip]
            target = base + which
            for dy, dx in offsets:
                for swap in (1, 0):
                    lane = 2 * chip_at(dy, dx) + (1 - core if swap else core)
                    copy = remote(
                        parts_even.at[which * count + lane], slot, dx_send, dx_recv.at[0], target, lane
                    )
                    if dy or dx or swap:
                        copy.start()
                    else:
                        pl.when(mine != which)(copy.start)

        gradient_phase(chosen, arrive, deliver)
        pltpu.make_async_copy(
            parts_even.at[mine * count + tensor],
            got_even.at[(2 * mine + core) * chips + chip],
            dx_recv.at[0],
        ).start()
        weight_phase()
        hand_over().wait_recv()
        wait_all(got_even, dx_recv.at[0])
        for place in range(4):
            total = got_even[place * chips].astype(F32)
            for slot in range(1, chips):
                total = total + got_even[place * chips + slot].astype(F32)
            part = quarter_columns(place)
            dx_ref[0, :, part] = (grad_own[:, part].astype(F32) + total).astype(BF16)
        wait_all(grad_full.at[pl.ds(0, 2 * (chips - 1) * block)], grad_send)
        wait_all(got_even.at[pl.ds(0, 2 * count - 1)], dx_send)

    pl.when(odd == 1)(odd_section)
    pl.when(odd == 0)(even_section)
    gather_sent(x_in, x_send)
    for copy in (send_version, send_probs, send_wo, send_wv):
        copy.wait_send()
    x_chain[4]()
    grad_chain[4]()
    for copy in (send_gv, send_go):
        copy.wait()


def store_kernel(dx, gv, go, dx_out, gv_out, go_out, sem):
    copies = [
        pltpu.make_async_copy(source, result, sem.at[index])
        for index, (source, result) in enumerate(((dx, dx_out), (gv, gv_out), (go, go_out)))
    ]
    for copy in copies:
        copy.start()
    for copy in copies:
        copy.wait()


def on_device(section_input, query, key_stash, incoming, version, w_value, w_out):
    count = lax.axis_size("tensor")
    shard, width = section_input.shape[1:]
    rows, tokens = query.shape[1:]
    half = width // 2
    quarter = half // 2
    heads = rows // HEAD_DIM
    hbm = pl.BlockSpec(memory_space=pltpu.HBM)
    local = pl.BlockSpec(memory_space=pltpu.VMEM)
    weight = pltpu.VMEM((2, 2 * rows, quarter), BF16)
    blocks = pltpu.VMEM((2 * count, shard, quarter), BF16)
    big_blocks = pltpu.VMEM((count, 2 * shard, quarter), BF16)
    full = pltpu.VMEM((2 * tokens, quarter), BF16)
    pair = pltpu.VMEM((2, rows, tokens), BF16)
    chain = [
        pltpu.VMEM((2, 2 * rows, tokens), F32),
        pltpu.VMEM((2, 2 * rows, tokens), BF16),
        pair,
        pltpu.VMEM((2, rows, tokens), F32),
        pair,
        pair,
        pltpu.VMEM((2 * rows, 2 * tokens), BF16),
    ]
    own = pltpu.VMEM((shard, width), BF16)
    result = pltpu.VMEM((rows, quarter), BF16)
    two = pltpu.VMEM((2, 2 * shard, quarter), BF16)
    dma = pltpu.SemaphoreType.DMA
    shapes = ((1, shard, width), (1, rows, half), (1, rows, half))
    results = pl.pallas_call(
        functools.partial(kernel, count),
        out_shape=tuple(pltpu.VMEM(shape, BF16) for shape in shapes),
        in_specs=[hbm] * 4 + [pl.BlockSpec(memory_space=pltpu.SMEM)] + [hbm] * 2,
        out_specs=(local, local, local),
        scratch_shapes=[
            weight, weight,
            pltpu.VMEM((rows, tokens), BF16),
            pltpu.VMEM((rows, tokens), BF16),
            pltpu.VMEM((2, heads, tokens, tokens), BF16),
            pltpu.VMEM((2, 8, 128), jnp.int32),
            blocks, blocks, full, full,
            *chain, *chain,
            full, big_blocks, blocks, blocks,
            two, two,
            pltpu.VMEM((2, 2, shard, quarter), BF16),
            pltpu.VMEM((4, shard, quarter), BF16),
            own, own, result, result,
            dma((5,)), dma((6,)), dma((6,)), dma((12,)), dma((12,)),
            dma, dma((2,)), dma, dma((2,)), dma, dma((2 * CUTS,)),
            dma((2 * CUTS,)), dma((2 * CUTS,)), dma, dma, dma, dma,
        ],
        compiler_params=pltpu.CompilerParams(
            collective_id=0, has_side_effects=True, vmem_limit_bytes=56 * 1024 * 1024
        ),
    )(section_input, query, key_stash, incoming, version, w_value, w_out)
    return pl.pallas_call(
        store_kernel,
        out_shape=tuple(jax.ShapeDtypeStruct(shape, BF16) for shape in shapes),
        in_specs=[local] * 3,
        out_specs=(hbm, hbm, hbm),
        scratch_shapes=[dma((3,))],
        compiler_params=pltpu.CompilerParams(vmem_limit_bytes=4 * 1024 * 1024),
    )(*results)


def solution(mesh):
    split = P("section", "tensor", None)
    weights = P("section", None, "tensor", None)
    return jax.shard_map(
        on_device,
        mesh=mesh,
        in_specs=(split, split, split, split, P("section"), weights, weights),
        out_specs=(split, split, split),
        check_vma=False,
    )
```

```python
import functools
import math

import jax
import jax.numpy as jnp
from jax import lax
from jax.experimental import pallas as pl
from jax.experimental.pallas import tpu as pltpu
from jax.sharding import PartitionSpec as P

HEAD_DIM = 96
CUTS = 2
BF16 = jnp.bfloat16
F32 = jnp.float32
MESH = pl.DeviceIdType.MESH


def dot(left, right, left_dim, right_dim):
    return lax.dot_general(
        left, right, (((left_dim,), (right_dim,)), ((), ())), preferred_element_type=F32
    )


def kernel(
    count,
    x_ref, query_ref, key_ref, incoming_ref, version_ref, wv_ref, wo_ref,
    dx_ref, gv_ref, go_ref,
    wv, wo, query, key, probs, versions,
    x_in, grad_in, x_full, grad_full,
    part_x, cast_x, sib_x, total_x, sent_x, got_x, context,
    part_g, cast_g, sib_g, total_g, sent_g, got_g, value_grad,
    parts_odd, got_odd, parts_even, got_even,
    reduced, shifted, pieces, assembled, row, grad_own, gv_sent, go_sent,
    ready_sem, load_sem, pair_send, pair_recv, sib_send, sib_recv,
    x_send, x_recv, grad_send, grad_recv, dx_send, dx_recv,
    shift_send, shift_recv, piece_send, piece_recv, own_send, own_recv,
):
    section = lax.axis_index("section")
    tensor = lax.axis_index("tensor")
    mine = lax.rem(section, 2)
    base = section - mine
    partner = base + 1 - mine
    odd = lax.rem(section // 2, 2)
    other = section + 2 - 4 * odd
    core = lax.rem(tensor, 2)
    chip = tensor // 2
    sibling = tensor + 1 - 2 * core
    rows = wv.shape[1] // 2
    quarter = wv.shape[2]
    half = 2 * quarter
    heads = rows // HEAD_DIM
    shard = grad_own.shape[0]
    tokens = count * shard
    chips = count // 2
    block = 2 * shard
    own_rows = pl.ds(pl.multiple_of(core * rows, 16), rows)
    sib_rows = pl.ds(pl.multiple_of((1 - core) * rows, 16), rows)

    offsets = [(dy, dx) for dx in (1, 0) for dy in sorted(range(chips // 2), key=lambda d: (-min(d, chips // 2 - d), d))]

    def chip_at(dy, dx):
        side = lax.rem(chip, 2)
        return 2 * lax.rem(chip // 2 + dy, chips // 2) + (1 - side if dx else side)

    def columns(side, which):
        return pl.ds(pl.multiple_of(side * half + which * quarter, 128), quarter)

    def remote(source, destination, send, recv, target, lane):
        return pltpu.make_async_remote_copy(
            src_ref=source,
            dst_ref=destination,
            send_sem=send,
            recv_sem=recv,
            device_id=(target, lane),
            device_id_type=MESH,
        )

    def to_partner(source, destination, index):
        return remote(
            source, destination, pair_send.at[index], pair_recv.at[index], partner, tensor
        )

    def to_sibling(source, destination, index):
        return remote(
            source, destination, sib_send.at[index], sib_recv.at[index], section, sibling
        )

    def wait_all(buffer, sem):
        pltpu.make_async_copy(buffer, buffer, sem).wait()

    loads = [
        pltpu.make_async_copy(query_ref.at[0], query, load_sem.at[0]),
        pltpu.make_async_copy(key_ref.at[0], key, load_sem.at[1]),
        pltpu.make_async_copy(
            wo_ref.at[0, :, :, columns(0, core)], wo.at[:, own_rows], load_sem.at[2]
        ),
        pltpu.make_async_copy(
            wv_ref.at[0, :, :, columns(0, core)], wv.at[:, own_rows], load_sem.at[3]
        ),
    ]
    load_incoming = pltpu.make_async_copy(incoming_ref.at[0], row, load_sem.at[4])
    load_x = pltpu.make_async_copy(x_ref.at[0], row, load_sem.at[4])
    pl.when(odd == 1)(load_incoming.start)
    pl.when(odd == 0)(load_x.start)
    barrier = pltpu.get_barrier_semaphore()

    def signal(target, lane):
        pl.semaphore_signal(barrier, inc=1, device_id=(target, lane), device_id_type=MESH)

    for dy, dx in offsets:
        place = chip_at(dy, dx)
        for swap in (1, 0):
            lane = 2 * place + (1 - core if swap else core)
            signal(partner, lane)
            if dy or dx or swap:
                signal(section, lane)
    pl.when(odd == 1)(lambda: signal(other, tensor))
    for load in loads:
        load.start()
    versions[mine] = jnp.full(versions.shape[1:], version_ref[0], jnp.int32)
    pl.semaphore_wait(barrier, 2 * count - odd)
    pl.when(odd == 0)(
        lambda: pl.semaphore_signal(
            ready_sem, inc=1, device_id=(other, tensor), device_id_type=MESH
        )
    )

    send_version = to_partner(versions.at[mine], versions.at[mine], 0)
    send_probs = to_partner(probs.at[mine], probs.at[mine], 1)
    send_wo = to_sibling(wo_ref.at[0, :, :, columns(0, 1 - core)], wo.at[:, own_rows], 0)
    send_wv = to_sibling(wv_ref.at[0, :, :, columns(0, 1 - core)], wv.at[:, own_rows], 1)

    def gather_start(source, buffer, send, recv):
        slot = buffer.at[mine * count + tensor]
        for dy, dx in offsets:
            for swap in (1, 0):
                lane_core = 1 - core if swap else core
                lane = 2 * chip_at(dy, dx) + lane_core
                remote(
                    source.at[:, columns(1 - mine, lane_core)], slot, send, recv.at[mine], partner, lane
                ).start()
        for dy, dx in offsets:
            for swap in (1, 0):
                if dy or dx or swap:
                    lane_core = 1 - core if swap else core
                    lane = 2 * chip_at(dy, dx) + lane_core
                    remote(
                        source.at[:, columns(mine, lane_core)], slot, send, recv.at[mine], section, lane
                    ).start()
        pltpu.make_async_copy(source.at[:, columns(mine, core)], slot, recv.at[mine]).start()

    def gather_wait(buffer, full, recv, which):
        wait_all(buffer.at[pl.ds(which * count, count)], recv.at[which])

        def step(i, carry):
            pair = buffer[pl.ds(which * count + 2 * i, 2)].astype(F32).reshape(block, quarter)
            start = pl.multiple_of(which * tokens + i * block, block)
            full[pl.ds(start, block), :] = pair.astype(BF16)
            return carry

        lax.fori_loop(0, chips, step, 0, unroll=True)

    def gather_sent(buffer, send):
        wait_all(buffer.at[pl.ds(0, 2 * count - 1)], send)

    def attention():
        send_version.start()
        send_wo.start()
        send_wv.start()
        loads[0].wait()
        loads[1].wait()
        line = lax.broadcasted_iota(jnp.int32, (tokens, tokens), 0)
        causal = lax.broadcasted_iota(jnp.int32, (tokens, tokens), 1) <= line
        for head in range(heads):
            part = slice(head * HEAD_DIM, (head + 1) * HEAD_DIM)
            scores = dot(query[part], key[part], 0, 0) * (1.0 / math.sqrt(HEAD_DIM))
            scores = jnp.where(causal, scores, -jnp.inf)
            expo = jnp.exp(scores - jnp.max(scores, axis=1, keepdims=True))
            attend = expo / jnp.sum(expo, axis=1, keepdims=True)
            probs[mine, head] = attend.astype(BF16)
        pl.when(odd == 0)(send_probs.start)
        for load in loads[2:]:
            load.wait()
        send_wo.wait_recv()
        send_wv.wait_recv()
        send_version.wait_recv()
        return [jnp.max(versions[which]) for which in range(2)]

    def token_rows(which):
        return slice(which * tokens, (which + 1) * tokens)

    def chain(weight, full, part, cast, sib, total, sent, got, out, side, first_sib, first_pair):
        def first_copy(which):
            return to_sibling(cast.at[which, sib_rows], sib.at[which], first_sib + which)

        def second_copy(which):
            return to_partner(sent.at[which], got.at[which], first_pair + which)

        def third_copy(which):
            place = out.at[own_rows, token_rows(which)]
            return to_sibling(place, place, first_sib + 2 + which)

        def first(which, version, pieces=None):
            if pieces is None:
                product = dot(weight[version], full[token_rows(which)], 1, 1)
            else:
                product = pieces(weight.at[version])
            part[which] = product
            cast[which] = product.astype(BF16)
            first_copy(which).start()

        def second(which):
            first_copy(which).wait_recv()
            chip_sum = part[which, own_rows] + sib[which].astype(F32)
            total[which] = chip_sum
            sent[which] = chip_sum.astype(BF16)
            second_copy(which).start()

        def third(which):
            second_copy(which).wait_recv()
            for head in range(heads):
                block_rows = slice(head * HEAD_DIM, (head + 1) * HEAD_DIM)
                whole = total[which, block_rows] + got[which, block_rows].astype(F32)
                mixed = dot(whole.astype(BF16), probs[which, head], 1, side)
                start = pl.multiple_of(core * rows + head * HEAD_DIM, 16)
                out[pl.ds(start, HEAD_DIM), token_rows(which)] = mixed.astype(BF16)
            third_copy(which).start()

        def last(which):
            third_copy(which).wait_recv()

        def sent_wait():
            for which in range(2):
                first_copy(which).wait_send()
                second_copy(which).wait_send()
                third_copy(which).wait_send()

        return first, second, third, last, sent_wait

    x_chain = chain(
        wv, x_full, part_x, cast_x, sib_x, total_x, sent_x, got_x, context, 1, 2, 2
    )
    grad_chain = chain(
        wo, grad_full, part_g, cast_g, sib_g, total_g, sent_g, got_g, value_grad, 0, 6, 4
    )

    def context_phase(chosen, before_third=lambda: None):
        first, second, third, last, _ = x_chain
        for which in range(2):
            gather_wait(x_in, x_full, x_recv, which)
            first(which, chosen[which])
        for which in range(2):
            second(which)
        before_third()
        for which in range(2):
            third(which)
        for which in range(2):
            last(which)

    def gradient_phase(chosen, arrive, deliver, before_third=lambda: None):
        first, second, third, last, _ = grad_chain
        def last_step(which):
            last(which)
            weight = wv.at[chosen[which]]
            deliver(
                which, lambda part: dot(value_grad[:, token_rows(which)], weight[:, part], 0, 0)
            )

        for which in range(2):
            first(which, chosen[which], arrive(which))
            second(which)
        before_third()
        third(0)
        last_step(0)
        third(1)
        last_step(1)

    send_gv = to_sibling(gv_sent, gv_ref.at[0, :, columns(0, core)], 10)
    send_go = to_sibling(go_sent, go_ref.at[0, :, columns(0, core)], 11)

    def weight_phase():
        for terms, full, kept, sent, send in (
            (value_grad, x_full, gv_ref, gv_sent, send_gv),
            (context, grad_full, go_ref, go_sent, send_go),
        ):
            sent[...] = dot(terms[sib_rows], full[...], 1, 0).astype(BF16)
            send.start()
            kept[0, :, columns(0, core)] = dot(terms[own_rows], full[...], 1, 0).astype(BF16)

    def chip_rows(which, place):
        return pl.ds(pl.multiple_of(which * tokens + place * block, block), block)

    def cut_columns(cut):
        return slice(cut * (quarter // CUTS), (cut + 1) * (quarter // CUTS))

    all_cuts = [(which, cut) for which in range(2) for cut in range(CUTS)]

    def shift(which, cut):
        place = which * CUTS + cut
        return remote(
            reduced.at[which, :, cut_columns(cut)], shifted.at[which, :, cut_columns(cut)],
            shift_send.at[place], shift_recv.at[place], other, tensor,
        )

    def hand_over():
        return remote(dx_ref.at[0], grad_own, own_send, own_recv, other, tensor)

    def quarter_columns(place):
        return slice(place * quarter, (place + 1) * quarter)

    def settle():
        gather_sent(x_in, x_send)
        for copy in (send_version, send_probs, send_wo, send_wv):
            copy.wait_send()
        x_chain[4]()
        grad_chain[4]()
        for copy in (send_gv, send_go):
            copy.wait()

    def odd_section():
        load_incoming.wait()
        gather_start(row, grad_in, grad_send, grad_recv)
        chosen = attention()

        def arrive(which):
            gather_wait(grad_in, grad_full, grad_recv, which)
            if which == 0:
                send_probs.start()

        def deliver(which, multiply):
            for cut in range(CUTS):
                parts_odd[token_rows(which), cut_columns(cut)] = multiply(cut_columns(cut)).astype(BF16)
                slot = got_odd.at[which * chips + chip, :, cut_columns(cut)]
                arrived = dx_recv.at[which * CUTS + cut]
                for dy, dx in offsets:
                    place = chip_at(dy, dx)
                    source = parts_odd.at[chip_rows(which, place), cut_columns(cut)]
                    if dy or dx:
                        remote(source, slot, dx_send, arrived, section, 2 * place + core).start()
                    else:
                        pltpu.make_async_copy(source, slot, arrived).start()

        gradient_phase(chosen, arrive, deliver, send_probs.wait_recv)
        pl.semaphore_wait(ready_sem, 1)
        for which, cut in all_cuts:
            part = cut_columns(cut)
            wait_all(
                got_odd.at[pl.ds(which * chips, chips), :, part], dx_recv.at[which * CUTS + cut]
            )
            total = got_odd[which * chips, :, part].astype(F32)
            for place in range(1, chips):
                total = total + got_odd[which * chips + place, :, part].astype(F32)
            total = total + grad_full[chip_rows(which, chip), part].astype(F32)
            reduced[which, :, part] = total.astype(BF16)
            shift(which, cut).start()
            pieces[which, :, :, part] = total.reshape(2, shard, quarter // CUTS).astype(BF16)
        gather_start(x_ref.at[0], x_in, x_send, x_recv)
        slot = assembled.at[2 * mine + core]
        pltpu.make_async_copy(pieces.at[mine, core], slot, piece_recv).start()
        for target, line, lane, lane_core in (
            (section, mine, sibling, 1 - core),
            (partner, 1 - mine, tensor, core),
            (partner, 1 - mine, sibling, 1 - core),
        ):
            remote(pieces.at[line, lane_core], slot, piece_send, piece_recv, target, lane).start()
        wait_all(assembled, piece_recv)
        for place in range(4):
            dx_ref[0, :, quarter_columns(place)] = assembled[place]
        hand_over().start()
        context_phase(chosen)
        weight_phase()
        gather_sent(grad_in, grad_send)
        wait_all(got_odd.at[pl.ds(0, 2 * chips - 2)], dx_send)
        for which, cut in all_cuts:
            shift(which, cut).wait_send()
        wait_all(assembled.at[pl.ds(0, 3)], piece_send)
        hand_over().wait_send()
        settle()

    def even_section():
        load_x.wait()
        gather_start(row, x_in, x_send, x_recv)
        chosen = attention()
        context_phase(chosen, send_probs.wait_recv)
        for which, cut in all_cuts:
            shift(which, cut).wait_recv()
            source = shifted.at[which, :, cut_columns(cut)]
            slot = grad_full.at[chip_rows(which, chip), cut_columns(cut)]
            for dy, dx in offsets:
                if dy or dx:
                    remote(
                        source, slot, grad_send, grad_recv.at[which * CUTS + cut],
                        section, 2 * chip_at(dy, dx) + core,
                    ).start()
                else:
                    pltpu.make_async_copy(source, slot, grad_recv.at[which * CUTS + cut]).start()

        def arrive(which):
            def pieces(weight):
                product = None
                for cut in range(CUTS):
                    part = cut_columns(cut)
                    wait_all(grad_full.at[token_rows(which), part], grad_recv.at[which * CUTS + cut])
                    terms = dot(weight[:, part], grad_full[token_rows(which), part], 1, 1)
                    product = terms if product is None else product + terms
                return product

            return pieces

        def deliver(which, multiply):
            product = multiply(slice(None))
            parts_even[which * count:(which + 1) * count] = product.reshape(
                count, shard, quarter
            ).astype(BF16)
            slot = got_even.at[(2 * mine + core) * chips + chip]
            target = base + which
            for dy, dx in offsets:
                for swap in (1, 0):
                    lane = 2 * chip_at(dy, dx) + (1 - core if swap else core)
                    copy = remote(
                        parts_even.at[which * count + lane], slot, dx_send, dx_recv.at[mine], target, lane
                    )
                    if dy or dx or swap:
                        copy.start()
                    else:
                        pl.when(mine != which)(copy.start)

        gradient_phase(chosen, arrive, deliver)
        pltpu.make_async_copy(
            parts_even.at[mine * count + tensor],
            got_even.at[(2 * mine + core) * chips + chip],
            dx_recv.at[mine],
        ).start()
        weight_phase()
        settle()
        wait_all(grad_full.at[pl.ds(0, 2 * (chips - 1) * block)], grad_send)
        hand_over().wait_recv()
        wait_all(got_even.at[pl.ds(0, 2 * count - 1)], dx_send)
        for side in (mine, 1 - mine):
            wait_all(got_even.at[pl.ds(side * count, count)], dx_recv.at[side])
            for lane_core in range(2):
                first = side * count + lane_core * chips
                total = got_even[first].astype(F32)
                for slot in range(1, chips):
                    total = total + got_even[first + slot].astype(F32)
                part = columns(side, lane_core)
                dx_ref[0, :, part] = (grad_own[:, part].astype(F32) + total).astype(BF16)

    pl.when(odd == 1)(odd_section)
    pl.when(odd == 0)(even_section)


def store_kernel(dx, gv, go, dx_out, gv_out, go_out, sem):
    copies = [
        pltpu.make_async_copy(source, result, sem.at[index])
        for index, (source, result) in enumerate(((dx, dx_out), (gv, gv_out), (go, go_out)))
    ]
    for copy in copies:
        copy.start()
    for copy in copies:
        copy.wait()


def on_device(section_input, query, key_stash, incoming, version, w_value, w_out):
    count = lax.axis_size("tensor")
    shard, width = section_input.shape[1:]
    rows, tokens = query.shape[1:]
    half = width // 2
    quarter = half // 2
    heads = rows // HEAD_DIM
    hbm = pl.BlockSpec(memory_space=pltpu.HBM)
    local = pl.BlockSpec(memory_space=pltpu.VMEM)
    weight = pltpu.VMEM((2, 2 * rows, quarter), BF16)
    blocks = pltpu.VMEM((2 * count, shard, quarter), BF16)
    big_blocks = pltpu.VMEM((count, 2 * shard, quarter), BF16)
    full = pltpu.VMEM((2 * tokens, quarter), BF16)
    pair = pltpu.VMEM((2, rows, tokens), BF16)
    chain = [
        pltpu.VMEM((2, 2 * rows, tokens), F32),
        pltpu.VMEM((2, 2 * rows, tokens), BF16),
        pair,
        pltpu.VMEM((2, rows, tokens), F32),
        pair,
        pair,
        pltpu.VMEM((2 * rows, 2 * tokens), BF16),
    ]
    own = pltpu.VMEM((shard, width), BF16)
    result = pltpu.VMEM((rows, quarter), BF16)
    two = pltpu.VMEM((2, 2 * shard, quarter), BF16)
    dma = pltpu.SemaphoreType.DMA
    shapes = ((1, shard, width), (1, rows, half), (1, rows, half))
    results = pl.pallas_call(
        functools.partial(kernel, count),
        out_shape=tuple(pltpu.VMEM(shape, BF16) for shape in shapes),
        in_specs=[hbm] * 4 + [pl.BlockSpec(memory_space=pltpu.SMEM)] + [hbm] * 2,
        out_specs=(local, local, local),
        scratch_shapes=[
            weight, weight,
            pltpu.VMEM((rows, tokens), BF16),
            pltpu.VMEM((rows, tokens), BF16),
            pltpu.VMEM((2, heads, tokens, tokens), BF16),
            pltpu.VMEM((2, 8, 128), jnp.int32),
            blocks, blocks, full, full,
            *chain, *chain,
            full, big_blocks, blocks, blocks,
            two, two,
            pltpu.VMEM((2, 2, shard, quarter), BF16),
            pltpu.VMEM((4, shard, quarter), BF16),
            own, own, result, result,
            pltpu.SemaphoreType.REGULAR,
            dma((5,)), dma((6,)), dma((6,)), dma((12,)), dma((12,)),
            dma, dma((2,)), dma, dma((2 * CUTS,)), dma, dma((2 * CUTS,)),
            dma((2 * CUTS,)), dma((2 * CUTS,)), dma, dma, dma, dma,
        ],
        compiler_params=pltpu.CompilerParams(
            collective_id=0, has_side_effects=True, vmem_limit_bytes=56 * 1024 * 1024
        ),
    )(section_input, query, key_stash, incoming, version, w_value, w_out)
    return pl.pallas_call(
        store_kernel,
        out_shape=tuple(jax.ShapeDtypeStruct(shape, BF16) for shape in shapes),
        in_specs=[local] * 3,
        out_specs=(hbm, hbm, hbm),
        scratch_shapes=[dma((3,))],
        compiler_params=pltpu.CompilerParams(vmem_limit_bytes=4 * 1024 * 1024),
    )(*results)


def solution(mesh):
    split = P("section", "tensor", None)
    weights = P("section", None, "tensor", None)
    return jax.shard_map(
        on_device,
        mesh=mesh,
        in_specs=(split, split, split, split, P("section"), weights, weights),
        out_specs=(split, split, split),
        check_vma=False,
    )
```

```python
import functools
import math

import jax
import jax.numpy as jnp
from jax import lax
from jax.experimental import pallas as pl
from jax.experimental.pallas import tpu as pltpu
from jax.sharding import PartitionSpec as P

HEAD_DIM = 96
CUTS = 2
BF16 = jnp.bfloat16
F32 = jnp.float32
MESH = pl.DeviceIdType.MESH


def dot(left, right, left_dim, right_dim):
    return lax.dot_general(
        left, right, (((left_dim,), (right_dim,)), ((), ())), preferred_element_type=F32
    )


def kernel(
    count,
    x_ref, query_ref, key_ref, incoming_ref, version_ref, wv_ref, wo_ref,
    dx_ref, gv_ref, go_ref,
    wv, wo, query, key, probs, versions,
    x_in, grad_in, x_full, grad_full,
    part_x, cast_x, sib_x, total_x, sent_x, got_x, context,
    part_g, cast_g, sib_g, total_g, sent_g, got_g, value_grad,
    parts_odd, got_odd, parts_even, got_even,
    reduced, shifted, pieces, assembled, row, grad_own, gv_sent, go_sent,
    ready_sem, load_sem, pair_send, pair_recv, sib_send, sib_recv,
    x_send, x_recv, grad_send, grad_recv, dx_send, dx_recv,
    shift_send, shift_recv, piece_send, piece_recv, own_send, own_recv,
):
    section = lax.axis_index("section")
    tensor = lax.axis_index("tensor")
    mine = lax.rem(section, 2)
    base = section - mine
    partner = base + 1 - mine
    odd = lax.rem(section // 2, 2)
    other = section + 2 - 4 * odd
    core = lax.rem(tensor, 2)
    chip = tensor // 2
    sibling = tensor + 1 - 2 * core
    rows = wv.shape[1] // 2
    quarter = wv.shape[2]
    half = 2 * quarter
    heads = rows // HEAD_DIM
    shard = grad_own.shape[0]
    tokens = count * shard
    chips = count // 2
    block = 2 * shard
    own_rows = pl.ds(pl.multiple_of(core * rows, 16), rows)
    sib_rows = pl.ds(pl.multiple_of((1 - core) * rows, 16), rows)

    offsets = [(dy, dx) for dx in (1, 0) for dy in sorted(range(chips // 2), key=lambda d: (-min(d, chips // 2 - d), d))]

    def chip_at(dy, dx):
        side = lax.rem(chip, 2)
        return 2 * lax.rem(chip // 2 + dy, chips // 2) + (1 - side if dx else side)

    def columns(side, which):
        return pl.ds(pl.multiple_of(side * half + which * quarter, 128), quarter)

    def remote(source, destination, send, recv, target, lane):
        return pltpu.make_async_remote_copy(
            src_ref=source,
            dst_ref=destination,
            send_sem=send,
            recv_sem=recv,
            device_id=(target, lane),
            device_id_type=MESH,
        )

    def to_partner(source, destination, index):
        return remote(
            source, destination, pair_send.at[index], pair_recv.at[index], partner, tensor
        )

    def to_sibling(source, destination, index):
        return remote(
            source, destination, sib_send.at[index], sib_recv.at[index], section, sibling
        )

    def wait_all(buffer, sem):
        pltpu.make_async_copy(buffer, buffer, sem).wait()

    loads = [
        pltpu.make_async_copy(query_ref.at[0], query, load_sem.at[0]),
        pltpu.make_async_copy(key_ref.at[0], key, load_sem.at[1]),
        pltpu.make_async_copy(
            wo_ref.at[0, :, :, columns(0, core)], wo.at[:, own_rows], load_sem.at[2]
        ),
        pltpu.make_async_copy(
            wv_ref.at[0, :, :, columns(0, core)], wv.at[:, own_rows], load_sem.at[3]
        ),
    ]
    load_incoming = pltpu.make_async_copy(incoming_ref.at[0], row, load_sem.at[4])
    load_x = pltpu.make_async_copy(x_ref.at[0], row, load_sem.at[4])
    pl.when(odd == 1)(load_incoming.start)
    pl.when(odd == 0)(load_x.start)
    barrier = pltpu.get_barrier_semaphore()

    def signal(target, lane):
        pl.semaphore_signal(barrier, inc=1, device_id=(target, lane), device_id_type=MESH)

    for dy, dx in offsets:
        place = chip_at(dy, dx)
        for swap in (1, 0):
            lane = 2 * place + (1 - core if swap else core)
            signal(partner, lane)
            if dy or dx or swap:
                signal(section, lane)
    pl.when(odd == 1)(lambda: signal(other, tensor))
    for load in loads:
        load.start()
    versions[mine] = jnp.full(versions.shape[1:], version_ref[0], jnp.int32)
    pl.semaphore_wait(barrier, 2 * count - odd)
    pl.when(odd == 0)(
        lambda: pl.semaphore_signal(
            ready_sem, inc=1, device_id=(other, tensor), device_id_type=MESH
        )
    )

    send_version = to_partner(versions.at[mine], versions.at[mine], 0)
    send_probs = to_partner(probs.at[mine], probs.at[mine], 1)
    send_wo = to_sibling(wo_ref.at[0, :, :, columns(0, 1 - core)], wo.at[:, own_rows], 0)
    send_wv = to_sibling(wv_ref.at[0, :, :, columns(0, 1 - core)], wv.at[:, own_rows], 1)

    def gather_start(source, buffer, send, recv):
        slot = buffer.at[mine * count + tensor]
        for dy, dx in offsets:
            for swap in (1, 0):
                lane_core = 1 - core if swap else core
                lane = 2 * chip_at(dy, dx) + lane_core
                remote(
                    source.at[:, columns(1 - mine, lane_core)], slot, send, recv.at[mine], partner, lane
                ).start()
        for dy, dx in offsets:
            for swap in (1, 0):
                if dy or dx or swap:
                    lane_core = 1 - core if swap else core
                    lane = 2 * chip_at(dy, dx) + lane_core
                    remote(
                        source.at[:, columns(mine, lane_core)], slot, send, recv.at[mine], section, lane
                    ).start()
        pltpu.make_async_copy(source.at[:, columns(mine, core)], slot, recv.at[mine]).start()

    def gather_wait(buffer, full, recv, which):
        wait_all(buffer.at[pl.ds(which * count, count)], recv.at[which])

        def step(i, carry):
            pair = buffer[pl.ds(which * count + 2 * i, 2)].astype(F32).reshape(block, quarter)
            start = pl.multiple_of(which * tokens + i * block, block)
            full[pl.ds(start, block), :] = pair.astype(BF16)
            return carry

        lax.fori_loop(0, chips, step, 0, unroll=True)

    def gather_sent(buffer, send):
        wait_all(buffer.at[pl.ds(0, 2 * count - 1)], send)

    def attention():
        send_version.start()
        send_wo.start()
        send_wv.start()
        loads[0].wait()
        loads[1].wait()
        line = lax.broadcasted_iota(jnp.int32, (tokens, tokens), 0)
        causal = lax.broadcasted_iota(jnp.int32, (tokens, tokens), 1) <= line
        for head in range(heads):
            part = slice(head * HEAD_DIM, (head + 1) * HEAD_DIM)
            scores = dot(query[part], key[part], 0, 0) * (1.0 / math.sqrt(HEAD_DIM))
            scores = jnp.where(causal, scores, -jnp.inf)
            expo = jnp.exp(scores - jnp.max(scores, axis=1, keepdims=True))
            attend = expo / jnp.sum(expo, axis=1, keepdims=True)
            probs[mine, head] = attend.astype(BF16)
        pl.when(odd == 0)(send_probs.start)
        for load in loads[2:]:
            load.wait()
        send_wo.wait_recv()
        send_wv.wait_recv()
        send_version.wait_recv()
        return [jnp.max(versions[which]) for which in range(2)]

    def token_rows(which):
        return slice(which * tokens, (which + 1) * tokens)

    def chain(weight, full, part, cast, sib, total, sent, got, out, side, first_sib, first_pair):
        def first_copy(which):
            return to_sibling(cast.at[which, sib_rows], sib.at[which], first_sib + which)

        def second_copy(which):
            return to_partner(sent.at[which], got.at[which], first_pair + which)

        def third_copy(which):
            place = out.at[own_rows, token_rows(which)]
            return to_sibling(place, place, first_sib + 2 + which)

        def first(which, version, pieces=None):
            if pieces is None:
                product = dot(weight[version], full[token_rows(which)], 1, 1)
            else:
                product = pieces(weight.at[version])
            part[which] = product
            cast[which] = product.astype(BF16)
            first_copy(which).start()

        def second(which):
            first_copy(which).wait_recv()
            chip_sum = part[which, own_rows] + sib[which].astype(F32)
            total[which] = chip_sum
            sent[which] = chip_sum.astype(BF16)
            second_copy(which).start()

        def third(which):
            second_copy(which).wait_recv()
            for head in range(heads):
                block_rows = slice(head * HEAD_DIM, (head + 1) * HEAD_DIM)
                whole = total[which, block_rows] + got[which, block_rows].astype(F32)
                mixed = dot(whole.astype(BF16), probs[which, head], 1, side)
                start = pl.multiple_of(core * rows + head * HEAD_DIM, 16)
                out[pl.ds(start, HEAD_DIM), token_rows(which)] = mixed.astype(BF16)
            third_copy(which).start()

        def last(which):
            third_copy(which).wait_recv()

        def sent_wait():
            for which in range(2):
                first_copy(which).wait_send()
                second_copy(which).wait_send()
                third_copy(which).wait_send()

        return first, second, third, last, sent_wait

    x_chain = chain(
        wv, x_full, part_x, cast_x, sib_x, total_x, sent_x, got_x, context, 1, 2, 2
    )
    grad_chain = chain(
        wo, grad_full, part_g, cast_g, sib_g, total_g, sent_g, got_g, value_grad, 0, 6, 4
    )

    def context_phase(chosen, before_third=lambda: None):
        first, second, third, last, _ = x_chain
        for which in range(2):
            gather_wait(x_in, x_full, x_recv, which)
            first(which, chosen[which])
        for which in range(2):
            second(which)
        before_third()
        for which in range(2):
            third(which)
        for which in range(2):
            last(which)

    def gradient_phase(chosen, arrive, deliver, before_third=lambda: None):
        first, second, third, last, _ = grad_chain
        def last_step(which):
            last(which)
            weight = wv.at[chosen[which]]
            turned = value_grad[:, token_rows(which)].T
            deliver(
                which, lambda part: dot(turned, weight[:, part], 1, 0)
            )

        for which in range(2):
            first(which, chosen[which], arrive(which))
            second(which)
        before_third()
        third(0)
        last_step(0)
        third(1)
        last_step(1)

    send_gv = to_sibling(gv_sent, gv_ref.at[0, :, columns(0, core)], 10)
    send_go = to_sibling(go_sent, go_ref.at[0, :, columns(0, core)], 11)

    def weight_phase():
        for terms, full, kept, sent, send in (
            (value_grad, x_full, gv_ref, gv_sent, send_gv),
            (context, grad_full, go_ref, go_sent, send_go),
        ):
            sent[...] = dot(terms[sib_rows], full[...], 1, 0).astype(BF16)
            send.start()
            kept[0, :, columns(0, core)] = dot(terms[own_rows], full[...], 1, 0).astype(BF16)

    def chip_rows(which, place):
        return pl.ds(pl.multiple_of(which * tokens + place * block, block), block)

    def cut_columns(cut):
        return slice(cut * (quarter // CUTS), (cut + 1) * (quarter // CUTS))

    all_cuts = [(which, cut) for which in range(2) for cut in range(CUTS)]

    def shift(which, cut):
        place = which * CUTS + cut
        return remote(
            reduced.at[which, :, cut_columns(cut)], shifted.at[which, :, cut_columns(cut)],
            shift_send.at[place], shift_recv.at[place], other, tensor,
        )

    def hand_over():
        return remote(dx_ref.at[0], grad_own, own_send, own_recv, other, tensor)

    def quarter_columns(place):
        return slice(place * quarter, (place + 1) * quarter)

    def settle():
        gather_sent(x_in, x_send)
        for copy in (send_version, send_probs, send_wo, send_wv):
            copy.wait_send()
        x_chain[4]()
        grad_chain[4]()
        for copy in (send_gv, send_go):
            copy.wait()

    def odd_section():
        load_incoming.wait()
        gather_start(row, grad_in, grad_send, grad_recv)
        chosen = attention()

        def arrive(which):
            gather_wait(grad_in, grad_full, grad_recv, which)
            if which == 0:
                send_probs.start()

        def deliver(which, multiply):
            for cut in range(CUTS):
                parts_odd[token_rows(which), cut_columns(cut)] = multiply(cut_columns(cut)).astype(BF16)
                slot = got_odd.at[which * chips + chip, :, cut_columns(cut)]
                arrived = dx_recv.at[which * CUTS + cut]
                for dy, dx in offsets:
                    place = chip_at(dy, dx)
                    source = parts_odd.at[chip_rows(which, place), cut_columns(cut)]
                    if dy or dx:
                        remote(source, slot, dx_send, arrived, section, 2 * place + core).start()
                    else:
                        pltpu.make_async_copy(source, slot, arrived).start()

        gradient_phase(chosen, arrive, deliver, send_probs.wait_recv)
        pl.semaphore_wait(ready_sem, 1)
        for which, cut in all_cuts:
            part = cut_columns(cut)
            wait_all(
                got_odd.at[pl.ds(which * chips, chips), :, part], dx_recv.at[which * CUTS + cut]
            )
            total = got_odd[which * chips, :, part].astype(F32)
            for place in range(1, chips):
                total = total + got_odd[which * chips + place, :, part].astype(F32)
            total = total + grad_full[chip_rows(which, chip), part].astype(F32)
            reduced[which, :, part] = total.astype(BF16)
            shift(which, cut).start()
            pieces[which, :, :, part] = total.reshape(2, shard, quarter // CUTS).astype(BF16)
        gather_start(x_ref.at[0], x_in, x_send, x_recv)
        slot = assembled.at[2 * mine + core]
        pltpu.make_async_copy(pieces.at[mine, core], slot, piece_recv).start()
        for target, line, lane, lane_core in (
            (section, mine, sibling, 1 - core),
            (partner, 1 - mine, tensor, core),
            (partner, 1 - mine, sibling, 1 - core),
        ):
            remote(pieces.at[line, lane_core], slot, piece_send, piece_recv, target, lane).start()
        wait_all(assembled, piece_recv)
        for place in range(4):
            dx_ref[0, :, quarter_columns(place)] = assembled[place]
        hand_over().start()
        context_phase(chosen)
        weight_phase()
        gather_sent(grad_in, grad_send)
        wait_all(got_odd.at[pl.ds(0, 2 * chips - 2)], dx_send)
        for which, cut in all_cuts:
            shift(which, cut).wait_send()
        wait_all(assembled.at[pl.ds(0, 3)], piece_send)
        hand_over().wait_send()
        settle()

    def even_section():
        load_x.wait()
        gather_start(row, x_in, x_send, x_recv)
        chosen = attention()
        context_phase(chosen, send_probs.wait_recv)
        for which, cut in all_cuts:
            shift(which, cut).wait_recv()
            source = shifted.at[which, :, cut_columns(cut)]
            slot = grad_full.at[chip_rows(which, chip), cut_columns(cut)]
            for dy, dx in offsets:
                if dy or dx:
                    remote(
                        source, slot, grad_send, grad_recv.at[which * CUTS + cut],
                        section, 2 * chip_at(dy, dx) + core,
                    ).start()
                else:
                    pltpu.make_async_copy(source, slot, grad_recv.at[which * CUTS + cut]).start()

        def arrive(which):
            def pieces(weight):
                product = None
                for cut in range(CUTS):
                    part = cut_columns(cut)
                    wait_all(grad_full.at[token_rows(which), part], grad_recv.at[which * CUTS + cut])
                    terms = dot(weight[:, part], grad_full[token_rows(which), part], 1, 1)
                    product = terms if product is None else product + terms
                return product

            return pieces

        def deliver(which, multiply):
            product = multiply(slice(None))
            parts_even[which * count:(which + 1) * count] = product.reshape(
                count, shard, quarter
            ).astype(BF16)
            slot = got_even.at[(2 * mine + core) * chips + chip]
            target = base + which
            for dy, dx in offsets:
                for swap in (1, 0):
                    lane = 2 * chip_at(dy, dx) + (1 - core if swap else core)
                    copy = remote(
                        parts_even.at[which * count + lane], slot, dx_send, dx_recv.at[mine], target, lane
                    )
                    if dy or dx or swap:
                        copy.start()
                    else:
                        pl.when(mine != which)(copy.start)

        gradient_phase(chosen, arrive, deliver)
        pltpu.make_async_copy(
            parts_even.at[mine * count + tensor],
            got_even.at[(2 * mine + core) * chips + chip],
            dx_recv.at[mine],
        ).start()
        weight_phase()
        settle()
        wait_all(grad_full.at[pl.ds(0, 2 * (chips - 1) * block)], grad_send)
        hand_over().wait_recv()
        wait_all(got_even.at[pl.ds(0, 2 * count - 1)], dx_send)
        for side in (mine, 1 - mine):
            wait_all(got_even.at[pl.ds(side * count, count)], dx_recv.at[side])
            for lane_core in range(2):
                first = side * count + lane_core * chips
                total = got_even[first].astype(F32)
                for slot in range(1, chips):
                    total = total + got_even[first + slot].astype(F32)
                part = columns(side, lane_core)
                dx_ref[0, :, part] = (grad_own[:, part].astype(F32) + total).astype(BF16)

    pl.when(odd == 1)(odd_section)
    pl.when(odd == 0)(even_section)


def store_kernel(dx, gv, go, dx_out, gv_out, go_out, sem):
    copies = [
        pltpu.make_async_copy(source, result, sem.at[index])
        for index, (source, result) in enumerate(((dx, dx_out), (gv, gv_out), (go, go_out)))
    ]
    for copy in copies:
        copy.start()
    for copy in copies:
        copy.wait()


def on_device(section_input, query, key_stash, incoming, version, w_value, w_out):
    count = lax.axis_size("tensor")
    shard, width = section_input.shape[1:]
    rows, tokens = query.shape[1:]
    half = width // 2
    quarter = half // 2
    heads = rows // HEAD_DIM
    hbm = pl.BlockSpec(memory_space=pltpu.HBM)
    local = pl.BlockSpec(memory_space=pltpu.VMEM)
    weight = pltpu.VMEM((2, 2 * rows, quarter), BF16)
    blocks = pltpu.VMEM((2 * count, shard, quarter), BF16)
    big_blocks = pltpu.VMEM((count, 2 * shard, quarter), BF16)
    full = pltpu.VMEM((2 * tokens, quarter), BF16)
    pair = pltpu.VMEM((2, rows, tokens), BF16)
    chain = [
        pltpu.VMEM((2, 2 * rows, tokens), F32),
        pltpu.VMEM((2, 2 * rows, tokens), BF16),
        pair,
        pltpu.VMEM((2, rows, tokens), F32),
        pair,
        pair,
        pltpu.VMEM((2 * rows, 2 * tokens), BF16),
    ]
    own = pltpu.VMEM((shard, width), BF16)
    result = pltpu.VMEM((rows, quarter), BF16)
    two = pltpu.VMEM((2, 2 * shard, quarter), BF16)
    dma = pltpu.SemaphoreType.DMA
    shapes = ((1, shard, width), (1, rows, half), (1, rows, half))
    results = pl.pallas_call(
        functools.partial(kernel, count),
        out_shape=tuple(pltpu.VMEM(shape, BF16) for shape in shapes),
        in_specs=[hbm] * 4 + [pl.BlockSpec(memory_space=pltpu.SMEM)] + [hbm] * 2,
        out_specs=(local, local, local),
        scratch_shapes=[
            weight, weight,
            pltpu.VMEM((rows, tokens), BF16),
            pltpu.VMEM((rows, tokens), BF16),
            pltpu.VMEM((2, heads, tokens, tokens), BF16),
            pltpu.VMEM((2, 8, 128), jnp.int32),
            blocks, blocks, full, full,
            *chain, *chain,
            full, big_blocks, blocks, blocks,
            two, two,
            pltpu.VMEM((2, 2, shard, quarter), BF16),
            pltpu.VMEM((4, shard, quarter), BF16),
            own, own, result, result,
            pltpu.SemaphoreType.REGULAR,
            dma((5,)), dma((6,)), dma((6,)), dma((12,)), dma((12,)),
            dma, dma((2,)), dma, dma((2 * CUTS,)), dma, dma((2 * CUTS,)),
            dma((2 * CUTS,)), dma((2 * CUTS,)), dma, dma, dma, dma,
        ],
        compiler_params=pltpu.CompilerParams(
            collective_id=0, has_side_effects=True, vmem_limit_bytes=56 * 1024 * 1024
        ),
    )(section_input, query, key_stash, incoming, version, w_value, w_out)
    return pl.pallas_call(
        store_kernel,
        out_shape=tuple(jax.ShapeDtypeStruct(shape, BF16) for shape in shapes),
        in_specs=[local] * 3,
        out_specs=(hbm, hbm, hbm),
        scratch_shapes=[dma((3,))],
        compiler_params=pltpu.CompilerParams(vmem_limit_bytes=4 * 1024 * 1024),
    )(*results)


def solution(mesh):
    split = P("section", "tensor", None)
    weights = P("section", None, "tensor", None)
    return jax.shard_map(
        on_device,
        mesh=mesh,
        in_specs=(split, split, split, split, P("section"), weights, weights),
        out_specs=(split, split, split),
        check_vma=False,
    )
```

```python
import functools
import math

import jax
import jax.numpy as jnp
from jax import lax
from jax.experimental import pallas as pl
from jax.experimental.pallas import tpu as pltpu
from jax.sharding import PartitionSpec as P

HEAD_DIM = 96
CUTS = 2
BF16 = jnp.bfloat16
F32 = jnp.float32
MESH = pl.DeviceIdType.MESH


def dot(left, right, left_dim, right_dim):
    return lax.dot_general(
        left, right, (((left_dim,), (right_dim,)), ((), ())), preferred_element_type=F32
    )


def kernel(
    count,
    x_ref, query_ref, key_ref, incoming_ref, version_ref, wv_ref, wo_ref,
    dx_ref, gv_ref, go_ref,
    wv, wo, query, key, probs, versions,
    x_in, grad_in, x_full, grad_full,
    part_x, cast_x, sib_x, total_x, sent_x, got_x, context,
    part_g, cast_g, sib_g, total_g, sent_g, got_g, value_grad,
    parts_odd, got_odd, parts_even, got_even,
    reduced, shifted, pieces, assembled, row, grad_own, gv_sent, go_sent,
    ready_sem, load_sem, pair_send, pair_recv, sib_send, sib_recv,
    x_send, x_recv, grad_send, grad_recv, dx_send, dx_recv,
    shift_send, shift_recv, piece_send, piece_recv, own_send, own_recv,
):
    section = lax.axis_index("section")
    tensor = lax.axis_index("tensor")
    mine = lax.rem(section, 2)
    base = section - mine
    partner = base + 1 - mine
    odd = lax.rem(section // 2, 2)
    other = section + 2 - 4 * odd
    core = lax.rem(tensor, 2)
    chip = tensor // 2
    sibling = tensor + 1 - 2 * core
    rows = wv.shape[1] // 2
    quarter = wv.shape[2]
    half = 2 * quarter
    heads = rows // HEAD_DIM
    shard = grad_own.shape[0]
    tokens = count * shard
    chips = count // 2
    block = 2 * shard
    own_rows = pl.ds(pl.multiple_of(core * rows, 16), rows)
    sib_rows = pl.ds(pl.multiple_of((1 - core) * rows, 16), rows)

    offsets = [(dy, dx) for dx in (1, 0) for dy in sorted(range(chips // 2), key=lambda d: (-min(d, chips // 2 - d), d))]

    def chip_at(dy, dx):
        side = lax.rem(chip, 2)
        return 2 * lax.rem(chip // 2 + dy, chips // 2) + (1 - side if dx else side)

    def columns(side, which):
        return pl.ds(pl.multiple_of(side * half + which * quarter, 128), quarter)

    def remote(source, destination, send, recv, target, lane):
        return pltpu.make_async_remote_copy(
            src_ref=source,
            dst_ref=destination,
            send_sem=send,
            recv_sem=recv,
            device_id=(target, lane),
            device_id_type=MESH,
        )

    def to_partner(source, destination, index):
        return remote(
            source, destination, pair_send.at[index], pair_recv.at[index], partner, tensor
        )

    def to_sibling(source, destination, index):
        return remote(
            source, destination, sib_send.at[index], sib_recv.at[index], section, sibling
        )

    def wait_all(buffer, sem):
        pltpu.make_async_copy(buffer, buffer, sem).wait()

    loads = [
        pltpu.make_async_copy(query_ref.at[0], query, load_sem.at[0]),
        pltpu.make_async_copy(key_ref.at[0], key, load_sem.at[1]),
        pltpu.make_async_copy(
            wo_ref.at[0, :, :, columns(0, core)], wo.at[:, own_rows], load_sem.at[2]
        ),
        pltpu.make_async_copy(
            wv_ref.at[0, :, :, columns(0, core)], wv.at[:, own_rows], load_sem.at[3]
        ),
    ]
    load_incoming = pltpu.make_async_copy(incoming_ref.at[0], row, load_sem.at[4])
    load_x = pltpu.make_async_copy(x_ref.at[0], row, load_sem.at[4])
    pl.when(odd == 1)(load_incoming.start)
    pl.when(odd == 0)(load_x.start)
    barrier = pltpu.get_barrier_semaphore()

    def signal(target, lane):
        pl.semaphore_signal(barrier, inc=1, device_id=(target, lane), device_id_type=MESH)

    for dy, dx in offsets:
        place = chip_at(dy, dx)
        for swap in (1, 0):
            lane = 2 * place + (1 - core if swap else core)
            signal(partner, lane)
            if dy or dx or swap:
                signal(section, lane)
    pl.when(odd == 1)(lambda: signal(other, tensor))
    for load in loads:
        load.start()
    versions[mine] = jnp.full(versions.shape[1:], version_ref[0], jnp.int32)
    pl.semaphore_wait(barrier, 2 * count - odd)
    pl.when(odd == 0)(
        lambda: pl.semaphore_signal(
            ready_sem, inc=1, device_id=(other, tensor), device_id_type=MESH
        )
    )

    send_version = to_partner(versions.at[mine], versions.at[mine], 0)
    send_probs = to_partner(probs.at[mine], probs.at[mine], 1)
    send_wo = to_sibling(wo_ref.at[0, :, :, columns(0, 1 - core)], wo.at[:, own_rows], 0)
    send_wv = to_sibling(wv_ref.at[0, :, :, columns(0, 1 - core)], wv.at[:, own_rows], 1)

    def gather_start(source, buffer, send, recv):
        slot = buffer.at[mine * count + tensor]
        for dy, dx in offsets:
            for swap in (1, 0):
                lane_core = 1 - core if swap else core
                lane = 2 * chip_at(dy, dx) + lane_core
                remote(
                    source.at[:, columns(1 - mine, lane_core)], slot, send, recv.at[mine], partner, lane
                ).start()
        for dy, dx in offsets:
            for swap in (1, 0):
                if dy or dx or swap:
                    lane_core = 1 - core if swap else core
                    lane = 2 * chip_at(dy, dx) + lane_core
                    remote(
                        source.at[:, columns(mine, lane_core)], slot, send, recv.at[mine], section, lane
                    ).start()
        pltpu.make_async_copy(source.at[:, columns(mine, core)], slot, recv.at[mine]).start()

    def gather_wait(buffer, full, recv, which):
        wait_all(buffer.at[pl.ds(which * count, count)], recv.at[which])

        def step(i, carry):
            pair = buffer[pl.ds(which * count + 2 * i, 2)].astype(F32).reshape(block, quarter)
            start = pl.multiple_of(which * tokens + i * block, block)
            full[pl.ds(start, block), :] = pair.astype(BF16)
            return carry

        lax.fori_loop(0, chips, step, 0, unroll=True)

    def gather_sent(buffer, send):
        wait_all(buffer.at[pl.ds(0, 2 * count - 1)], send)

    def attention():
        send_version.start()
        send_wo.start()
        send_wv.start()
        loads[0].wait()
        loads[1].wait()
        line = lax.broadcasted_iota(jnp.int32, (tokens, tokens), 0)
        causal = lax.broadcasted_iota(jnp.int32, (tokens, tokens), 1) <= line
        for head in range(heads):
            part = slice(head * HEAD_DIM, (head + 1) * HEAD_DIM)
            scores = dot(query[part], key[part], 0, 0) * (1.0 / math.sqrt(HEAD_DIM))
            scores = jnp.where(causal, scores, -jnp.inf)
            expo = jnp.exp(scores - jnp.max(scores, axis=1, keepdims=True))
            attend = expo / jnp.sum(expo, axis=1, keepdims=True)
            probs[mine, head] = attend.astype(BF16)
        pl.when(odd == 0)(send_probs.start)
        for load in loads[2:]:
            load.wait()
        send_wo.wait_recv()
        send_wv.wait_recv()
        send_version.wait_recv()
        return [jnp.max(versions[which]) for which in range(2)]

    def token_rows(which):
        return slice(which * tokens, (which + 1) * tokens)

    def chain(weight, full, part, cast, sib, total, sent, got, out, side, first_sib, first_pair):
        def first_copy(which):
            return to_sibling(cast.at[which, sib_rows], sib.at[which], first_sib + which)

        def second_copy(which):
            return to_partner(sent.at[which], got.at[which], first_pair + which)

        def third_copy(which):
            place = out.at[own_rows, token_rows(which)]
            return to_sibling(place, place, first_sib + 2 + which)

        def first(which, version, pieces=None):
            if pieces is None:
                product = dot(weight[version], full[token_rows(which)], 1, 1)
            else:
                product = pieces(weight.at[version])
            part[which] = product
            cast[which] = product.astype(BF16)
            first_copy(which).start()

        def second(which):
            first_copy(which).wait_recv()
            chip_sum = part[which, own_rows] + sib[which].astype(F32)
            total[which] = chip_sum
            sent[which] = chip_sum.astype(BF16)
            second_copy(which).start()

        def third(which):
            second_copy(which).wait_recv()
            for head in range(heads):
                block_rows = slice(head * HEAD_DIM, (head + 1) * HEAD_DIM)
                whole = total[which, block_rows] + got[which, block_rows].astype(F32)
                mixed = dot(whole.astype(BF16), probs[which, head], 1, side)
                start = pl.multiple_of(core * rows + head * HEAD_DIM, 16)
                out[pl.ds(start, HEAD_DIM), token_rows(which)] = mixed.astype(BF16)
            third_copy(which).start()

        def last(which):
            third_copy(which).wait_recv()

        def sent_wait():
            for which in range(2):
                first_copy(which).wait_send()
                second_copy(which).wait_send()
                third_copy(which).wait_send()

        return first, second, third, last, sent_wait

    x_chain = chain(
        wv, x_full, part_x, cast_x, sib_x, total_x, sent_x, got_x, context, 1, 2, 2
    )
    grad_chain = chain(
        wo, grad_full, part_g, cast_g, sib_g, total_g, sent_g, got_g, value_grad, 0, 6, 4
    )

    def context_phase(chosen, before_third=lambda: None):
        first, second, third, last, _ = x_chain
        for which in range(2):
            gather_wait(x_in, x_full, x_recv, which)
            first(which, chosen[which])
        for which in range(2):
            second(which)
        before_third()
        for which in range(2):
            third(which)
        for which in range(2):
            last(which)

    def gradient_phase(chosen, arrive, deliver, before_third=lambda: None):
        first, second, third, last, _ = grad_chain
        def last_step(which):
            last(which)
            weight = wv.at[chosen[which]]
            turned = value_grad[:, token_rows(which)].T
            deliver(
                which, lambda part: dot(turned, weight[:, part], 1, 0)
            )

        for which in range(2):
            first(which, chosen[which], arrive(which))
            second(which)
        before_third()
        third(0)
        last_step(0)
        third(1)
        last_step(1)

    send_gv = to_sibling(gv_sent, gv_ref.at[0, :, columns(0, core)], 10)
    send_go = to_sibling(go_sent, go_ref.at[0, :, columns(0, core)], 11)

    def weight_phase():
        for terms, full, kept, sent, send in (
            (value_grad, x_full, gv_ref, gv_sent, send_gv),
            (context, grad_full, go_ref, go_sent, send_go),
        ):
            sent[...] = dot(terms[sib_rows], full[...], 1, 0).astype(BF16)
            send.start()
            kept[0, :, columns(0, core)] = dot(terms[own_rows], full[...], 1, 0).astype(BF16)

    def chip_rows(which, place):
        return pl.ds(pl.multiple_of(which * tokens + place * block, block), block)

    def cut_columns(cut):
        return slice(cut * (quarter // CUTS), (cut + 1) * (quarter // CUTS))

    all_cuts = [(which, cut) for which in range(2) for cut in range(CUTS)]

    def shift(which, cut):
        place = which * CUTS + cut
        return remote(
            reduced.at[which, :, cut_columns(cut)], shifted.at[which, :, cut_columns(cut)],
            shift_send.at[place], shift_recv.at[place], other, tensor,
        )

    def hand_over():
        return remote(dx_ref.at[0], grad_own, own_send, own_recv, other, tensor)

    def quarter_columns(place):
        return slice(place * quarter, (place + 1) * quarter)

    def settle():
        gather_sent(x_in, x_send)
        for copy in (send_version, send_probs, send_wo, send_wv):
            copy.wait_send()
        x_chain[4]()
        grad_chain[4]()
        for copy in (send_gv, send_go):
            copy.wait()

    def odd_section():
        load_incoming.wait()
        gather_start(row, grad_in, grad_send, grad_recv)
        chosen = attention()

        def arrive(which):
            gather_wait(grad_in, grad_full, grad_recv, which)
            if which == 0:
                send_probs.start()

        def deliver(which, multiply):
            for cut in range(CUTS):
                parts_odd[token_rows(which), cut_columns(cut)] = multiply(cut_columns(cut)).astype(BF16)
                slot = got_odd.at[which * chips + chip, :, cut_columns(cut)]
                arrived = dx_recv.at[which * CUTS + cut]
                for dy, dx in offsets:
                    place = chip_at(dy, dx)
                    source = parts_odd.at[chip_rows(which, place), cut_columns(cut)]
                    if dy or dx:
                        remote(source, slot, dx_send, arrived, section, 2 * place + core).start()
                    else:
                        pltpu.make_async_copy(source, slot, arrived).start()

        gradient_phase(chosen, arrive, deliver, send_probs.wait_recv)
        pl.semaphore_wait(ready_sem, 1)
        for which, cut in all_cuts:
            part = cut_columns(cut)
            wait_all(
                got_odd.at[pl.ds(which * chips, chips), :, part], dx_recv.at[which * CUTS + cut]
            )
            total = got_odd[which * chips, :, part].astype(F32)
            for place in range(1, chips):
                total = total + got_odd[which * chips + place, :, part].astype(F32)
            total = total + grad_full[chip_rows(which, chip), part].astype(F32)
            reduced[which, :, part] = total.astype(BF16)
            shift(which, cut).start()
            pieces[which, :, :, part] = total.reshape(2, shard, quarter // CUTS).astype(BF16)
        gather_start(x_ref.at[0], x_in, x_send, x_recv)
        slot = assembled.at[2 * mine + core]
        pltpu.make_async_copy(pieces.at[mine, core], slot, piece_recv).start()
        for target, line, lane, lane_core in (
            (section, mine, sibling, 1 - core),
            (partner, 1 - mine, tensor, core),
            (partner, 1 - mine, sibling, 1 - core),
        ):
            remote(pieces.at[line, lane_core], slot, piece_send, piece_recv, target, lane).start()
        wait_all(assembled, piece_recv)
        for place in range(4):
            dx_ref[0, :, quarter_columns(place)] = assembled[place]
        hand_over().start()
        context_phase(chosen)
        weight_phase()
        gather_sent(grad_in, grad_send)
        wait_all(got_odd.at[pl.ds(0, 2 * chips - 2)], dx_send)
        for which, cut in all_cuts:
            shift(which, cut).wait_send()
        wait_all(assembled.at[pl.ds(0, 3)], piece_send)
        hand_over().wait_send()
        settle()

    def even_section():
        load_x.wait()
        gather_start(row, x_in, x_send, x_recv)
        chosen = attention()
        context_phase(chosen, send_probs.wait_recv)
        for which, cut in all_cuts:
            shift(which, cut).wait_recv()
            source = shifted.at[which, :, cut_columns(cut)]
            slot = grad_full.at[chip_rows(which, chip), cut_columns(cut)]
            for dy, dx in offsets:
                if dy or dx:
                    remote(
                        source, slot, grad_send, grad_recv.at[which * CUTS + cut],
                        section, 2 * chip_at(dy, dx) + core,
                    ).start()
                else:
                    pltpu.make_async_copy(source, slot, grad_recv.at[which * CUTS + cut]).start()

        def arrive(which):
            def pieces(weight):
                product = None
                for cut in range(CUTS):
                    part = cut_columns(cut)
                    wait_all(grad_full.at[token_rows(which), part], grad_recv.at[which * CUTS + cut])
                    terms = dot(weight[:, part], grad_full[token_rows(which), part], 1, 1)
                    product = terms if product is None else product + terms
                return product

            return pieces

        def deliver(which, multiply):
            product = multiply(slice(None))
            parts_even[which * count:(which + 1) * count] = product.reshape(
                count, shard, quarter
            ).astype(BF16)
            slot = got_even.at[(2 * mine + core) * chips + chip]
            target = base + which
            for dy, dx in offsets:
                for swap in (1, 0):
                    lane = 2 * chip_at(dy, dx) + (1 - core if swap else core)
                    copy = remote(
                        parts_even.at[which * count + lane], slot, dx_send, dx_recv.at[mine], target, lane
                    )
                    if dy or dx or swap:
                        copy.start()
                    else:
                        pl.when(mine != which)(copy.start)

        gradient_phase(chosen, arrive, deliver)
        pltpu.make_async_copy(
            parts_even.at[mine * count + tensor],
            got_even.at[(2 * mine + core) * chips + chip],
            dx_recv.at[mine],
        ).start()
        weight_phase()
        settle()
        wait_all(grad_full.at[pl.ds(0, 2 * (chips - 1) * block)], grad_send)
        hand_over().wait_recv()
        wait_all(got_even.at[pl.ds(0, 2 * count - 1)], dx_send)
        for side in (0, 1):
            wait_all(got_even.at[pl.ds(side * count, count)], dx_recv.at[side])
            for lane_core in range(2):
                first = side * count + lane_core * chips
                total = got_even[first].astype(F32)
                for slot in range(1, chips):
                    total = total + got_even[first + slot].astype(F32)
                part = quarter_columns(2 * side + lane_core)
                dx_ref[0, :, part] = (grad_own[:, part].astype(F32) + total).astype(BF16)

    pl.when(odd == 1)(odd_section)
    pl.when(odd == 0)(even_section)


def store_kernel(dx, gv, go, dx_out, gv_out, go_out, sem):
    copies = [
        pltpu.make_async_copy(source, result, sem.at[index])
        for index, (source, result) in enumerate(((dx, dx_out), (gv, gv_out), (go, go_out)))
    ]
    for copy in copies:
        copy.start()
    for copy in copies:
        copy.wait()


def on_device(section_input, query, key_stash, incoming, version, w_value, w_out):
    count = lax.axis_size("tensor")
    shard, width = section_input.shape[1:]
    rows, tokens = query.shape[1:]
    half = width // 2
    quarter = half // 2
    heads = rows // HEAD_DIM
    hbm = pl.BlockSpec(memory_space=pltpu.HBM)
    local = pl.BlockSpec(memory_space=pltpu.VMEM)
    weight = pltpu.VMEM((2, 2 * rows, quarter), BF16)
    blocks = pltpu.VMEM((2 * count, shard, quarter), BF16)
    big_blocks = pltpu.VMEM((count, 2 * shard, quarter), BF16)
    full = pltpu.VMEM((2 * tokens, quarter), BF16)
    pair = pltpu.VMEM((2, rows, tokens), BF16)
    chain = [
        pltpu.VMEM((2, 2 * rows, tokens), F32),
        pltpu.VMEM((2, 2 * rows, tokens), BF16),
        pair,
        pltpu.VMEM((2, rows, tokens), F32),
        pair,
        pair,
        pltpu.VMEM((2 * rows, 2 * tokens), BF16),
    ]
    own = pltpu.VMEM((shard, width), BF16)
    result = pltpu.VMEM((rows, quarter), BF16)
    two = pltpu.VMEM((2, 2 * shard, quarter), BF16)
    dma = pltpu.SemaphoreType.DMA
    shapes = ((1, shard, width), (1, rows, half), (1, rows, half))
    results = pl.pallas_call(
        functools.partial(kernel, count),
        out_shape=tuple(pltpu.VMEM(shape, BF16) for shape in shapes),
        in_specs=[hbm] * 4 + [pl.BlockSpec(memory_space=pltpu.SMEM)] + [hbm] * 2,
        out_specs=(local, local, local),
        scratch_shapes=[
            weight, weight,
            pltpu.VMEM((rows, tokens), BF16),
            pltpu.VMEM((rows, tokens), BF16),
            pltpu.VMEM((2, heads, tokens, tokens), BF16),
            pltpu.VMEM((2, 8, 128), jnp.int32),
            blocks, blocks, full, full,
            *chain, *chain,
            full, big_blocks, blocks, blocks,
            two, two,
            pltpu.VMEM((2, 2, shard, quarter), BF16),
            pltpu.VMEM((4, shard, quarter), BF16),
            own, own, result, result,
            pltpu.SemaphoreType.REGULAR,
            dma((5,)), dma((6,)), dma((6,)), dma((12,)), dma((12,)),
            dma, dma((2,)), dma, dma((2 * CUTS,)), dma, dma((2 * CUTS,)),
            dma((2 * CUTS,)), dma((2 * CUTS,)), dma, dma, dma, dma,
        ],
        compiler_params=pltpu.CompilerParams(
            collective_id=0, has_side_effects=True, vmem_limit_bytes=56 * 1024 * 1024
        ),
    )(section_input, query, key_stash, incoming, version, w_value, w_out)
    return pl.pallas_call(
        store_kernel,
        out_shape=tuple(jax.ShapeDtypeStruct(shape, BF16) for shape in shapes),
        in_specs=[local] * 3,
        out_specs=(hbm, hbm, hbm),
        scratch_shapes=[dma((3,))],
        compiler_params=pltpu.CompilerParams(vmem_limit_bytes=4 * 1024 * 1024),
    )(*results)


def solution(mesh):
    split = P("section", "tensor", None)
    weights = P("section", None, "tensor", None)
    return jax.shard_map(
        on_device,
        mesh=mesh,
        in_specs=(split, split, split, split, P("section"), weights, weights),
        out_specs=(split, split, split),
        check_vma=False,
    )
```
